32 devices in a mesh: row: 4 (over z_hi, core), col: 4 (over y, x), seq: 2 (over z_lo).
Axes of the slice: x: 2, y: 2, z: 4 (z_hi: 2, z_lo: 2; z = z_hi * 2 + z_lo), core: 2. Of those that a mesh axis runs over, the one named last changes fastest.
Arguments:
- alignment: bfloat16 [64, 128, 256], P('seq', ('row', 'col')), may hold values from -6 to 6
- left_weight: bfloat16 [256, 32], replicated, may hold values from -0.375 to 0.375
- right_weight: bfloat16 [256, 32], replicated, may hold values from -0.375 to 0.375
- out_weight: bfloat16 [1024, 128], replicated, may hold values from -0.1875 to 0.1875
- out_bias: float32 [128], replicated, may hold values from -3 to 3
- cotangent: bfloat16 [128, 128, 128], P(('row', 'seq'), 'col'), may hold values from -6 to 6
Outputs:
- pair_update: bfloat16 [128, 128, 128], P(('row', 'seq'), 'col')
- alignment_grad: float32 [64, 128, 256], P('seq', ('row', 'col'))
- left_weight_grad: float32 [256, 32], replicated
- right_weight_grad: float32 [256, 32], replicated
- out_weight_grad: float32 [1024, 128], replicated
The draws below stay inside these ranges and needn't reach their ends.
All inputs are finite; a program needn't handle non-finite values.
Results may differ from the reference program's by a relative error of at most 0.02.
Values may be sent and summed in bfloat16 or wider, within the bound.
A program may use at most 64 MiB of HBM per device.

```python
import math
import jax
import jax.numpy as jnp
from jax import lax

CM = 256
CP = 32
CZ = 128
SEQS = 64
RESIDUES = 128


def shard_levels(key, shape, pieces, smallest, high):
    loudness, own = 1.0, jax.random.fold_in(key, 6)
    for dim, shards_of in pieces:
        steps = jnp.exp(jax.random.uniform(jax.random.fold_in(own, dim), (shards_of,), jnp.float32, smallest / len(pieces), high / len(pieces)))
        loudness = loudness * jnp.repeat(steps, shape[dim] // shards_of).reshape([-1 if axis == dim else 1 for axis in range(len(shape))])
    return loudness


def centred(own_key, shape, width, most, pieces=(), held_as=jnp.bfloat16):
    result = width * jax.random.normal(own_key, shape, jnp.float32)
    if pieces:
        result = result * shard_levels(own_key, shape, pieces, -0.22, 0.18)
    return jnp.clip(result, -most, most).astype(held_as)


def setup_inputs(seed: int = 0) -> dict:
    key_list = jax.random.split(jax.random.key(seed), 7)
    alignment = centred(key_list[0], (SEQS, RESIDUES, CM), 1.0, 6.0, ((0, 2), (1, 16)))
    left_weight = centred(key_list[1], (CM, CP), CM ** -0.5, 0.375)
    right_weight = centred(key_list[2], (CM, CP), CM ** -0.5, 0.375)
    out_weight = centred(key_list[3], (CP * CP, CZ), (CP * CP) ** -0.5, 0.1875)
    out_bias = centred(key_list[4], (CZ,), 0.5, 3.0, (), jnp.float32)
    cotangent = centred(key_list[5], (RESIDUES, RESIDUES, CZ), 1.0, 6.0, ((0, 8), (1, 4)))
    return dict(alignment=alignment, left_weight=left_weight, right_weight=right_weight, out_weight=out_weight, out_bias=out_bias, cotangent=cotangent)


def reference(alignment, left_weight, right_weight, out_weight, out_bias, cotangent):
    values = alignment.astype(jnp.float32)
    center = values - lax.optimization_barrier(jnp.mean(values, axis=2, keepdims=True))
    invstd = lax.rsqrt(lax.optimization_barrier(jnp.mean(center * center, axis=2, keepdims=True)) + 1e-05)
    scaled = center * invstd
    normed = scaled.astype(jnp.bfloat16)
    flat_normed = normed.reshape(SEQS * RESIDUES, CM)
    left = jnp.dot(flat_normed, left_weight, preferred_element_type=jnp.float32).astype(jnp.bfloat16)
    right = jnp.dot(flat_normed, right_weight, preferred_element_type=jnp.float32).astype(jnp.bfloat16)
    left_full = left.reshape(SEQS, RESIDUES, CP).astype(jnp.float32)
    right_full = right.reshape(SEQS, RESIDUES, CP).astype(jnp.float32)
    block_rows = math.gcd(RESIDUES, 32)
    block_count = RESIDUES // block_rows
    inverse = 1.0 / SEQS

    def one_block(carry, index):
        wout_total, right_total = carry
        start = (index * block_rows).astype(jnp.int32)
        left_piece = lax.dynamic_slice_in_dim(left_full, start, block_rows, 1)
        cot_flat = lax.dynamic_slice_in_dim(cotangent, start, block_rows, 0).reshape(block_rows * RESIDUES, CZ)
        outer = jnp.einsum('sic,sjd->ijcd', left_piece, right_full) * inverse
        outer_flat = outer.astype(jnp.bfloat16).reshape(block_rows * RESIDUES, CP * CP)
        pair = (jnp.dot(outer_flat, out_weight, preferred_element_type=jnp.float32) + out_bias).astype(jnp.bfloat16)
        wout_total = wout_total + lax.dot_general(outer_flat, cot_flat, (((0,), (0,)), ((), ())), preferred_element_type=jnp.float32)
        outer_grad = (jnp.dot(cot_flat, out_weight.T, preferred_element_type=jnp.float32) * inverse).astype(jnp.bfloat16)
        outer_grad = lax.optimization_barrier(outer_grad)
        outer_grad = outer_grad.astype(jnp.float32).reshape(block_rows, RESIDUES, CP, CP)
        left_part = jnp.einsum('ijcd,sjd->sic', outer_grad, right_full)
        right_total = right_total + jnp.einsum('ijcd,sic->sjd', outer_grad, left_piece)
        return ((wout_total, right_total), (pair, left_part))
    init = (jnp.zeros((CP * CP, CZ), jnp.float32), jnp.zeros((SEQS, RESIDUES, CP), jnp.float32))
    (wout_total, right_total), (pairs, left_parts) = lax.scan(one_block, init, jnp.arange(block_count, dtype=jnp.int32))
    pair_update = pairs.reshape(RESIDUES, RESIDUES, CZ)
    left_grad = left_parts.transpose(1, 0, 2, 3).reshape(SEQS * RESIDUES, CP).astype(jnp.bfloat16)
    right_grad = right_total.reshape(SEQS * RESIDUES, CP).astype(jnp.bfloat16)
    left_weight_grad = lax.dot_general(flat_normed, left_grad, (((0,), (0,)), ((), ())), preferred_element_type=jnp.float32) / RESIDUES
    right_weight_grad = lax.dot_general(flat_normed, right_grad, (((0,), (0,)), ((), ())), preferred_element_type=jnp.float32) / RESIDUES
    normed_grad = jnp.dot(left_grad, left_weight.T, preferred_element_type=jnp.float32) + jnp.dot(right_grad, right_weight.T, preferred_element_type=jnp.float32)
    normed_grad = normed_grad.reshape(SEQS, RESIDUES, CM)
    mean_grad = lax.optimization_barrier(jnp.mean(normed_grad, axis=2, keepdims=True))
    mean_cross = lax.optimization_barrier(jnp.mean(normed_grad * scaled, axis=2, keepdims=True))
    alignment_grad = invstd * (normed_grad - mean_grad - scaled * mean_cross)
    return (pair_update, alignment_grad, left_weight_grad, right_weight_grad, wout_total / RESIDUES)
```

```python
import functools

import jax
import jax.numpy as jnp
from jax import lax
from jax.experimental import pallas as pl
from jax.experimental.pallas import tpu as pltpu
from jax.sharding import PartitionSpec as P

F32 = jnp.float32
BF16 = jnp.bfloat16
MESH = pl.DeviceIdType.MESH
LANES = 128
DG = 8


def nn(a, b):
    return lax.dot_general(a, b, (((1,), (0,)), ((), ())), preferred_element_type=F32)


def nt(a, b):
    return lax.dot_general(a, b, (((1,), (1,)), ((), ())), preferred_element_type=F32)


def log2(n):
    assert n & (n - 1) == 0
    return n.bit_length() - 1


def div(x, n):
    return lax.shift_right_logical(x, jnp.int32(log2(n)))


def mod(x, n):
    return x & (n - 1)


def iota(shape, dim):
    return lax.broadcasted_iota(jnp.int32, shape, dim)


def zero_one(mask):
    return jnp.where(mask, 1.0, 0.0).astype(BF16)


def kernel(
    dims,
    align_ref,
    lw_ref,
    rw_ref,
    wout_ref,
    bias_ref,
    cot_ref,
    pair_ref,
    agrad_ref,
    wg_ref,
    wog_ref,
    s_l,
    s_r,
    l3,
    r3,
    rbd,
    og2,
    ot,
    wf,
    w2,
    s_lg,
    s_rg,
    r_lg,
    r_rg,
    s_w,
    r_w,
    g_w,
    s_v,
    r_v,
    g_v,
    sl_sem,
    rl_sem,
    sr_sem,
    rr_sem,
    slg_sem,
    rlg_sem,
    srg_sem,
    rrg_sem,
    w_sem,
    v_sem,
):
    R, C, SQ, SL, RB, CP, rows, cols = dims
    N = R * C * SQ
    I4 = LANES // SL
    GPB = RB // I4
    G = rows // I4
    NKB = rows // RB
    NB = cols // RB
    IJ = I4 * cols
    DH = CP // DG
    PW = DG * RB
    CH = DG * IJ
    KS = SQ * I4 * SL
    inverse = 1.0 / (SQ * SL)
    residues = RB * R * C

    r = lax.axis_index("row")
    c = lax.axis_index("col")
    s = lax.axis_index("seq")
    me = (r * C + c) * SQ + s

    def dev(lin):
        return (lin // (C * SQ), (lin // SQ) % C, lin % SQ)

    barrier = pltpu.get_barrier_semaphore()

    def greet(k, carry):
        pl.semaphore_signal(barrier, inc=1, device_id=dev((me + k) % N), device_id_type=MESH)
        return carry

    lax.fori_loop(1, N, greet, 0)

    values = align_ref[...].astype(F32)
    center = values - jnp.mean(values, axis=1, keepdims=True)
    invstd = lax.rsqrt(jnp.mean(center * center, axis=1, keepdims=True) + 1e-05)
    scaled = center * invstd
    normed = scaled.astype(BF16)
    M = SL * RB
    row_m, col_m = iota((M, M), 0), iota((M, M), 1)
    perm = zero_one(col_m == mod(row_m, SL) * RB + div(row_m, SL))
    normed_rs = nn(perm, normed).astype(BF16)
    eye = zero_one(iota((CP, CP), 0) == iota((CP, CP), 1))
    lw_t = nt(eye, lw_ref[...]).astype(BF16)
    left_t = nt(lw_t, normed_rs).astype(BF16)
    for h in range(GPB):
        s_l[h] = left_t[:, h * LANES : (h + 1) * LANES]
    spread = zero_one(iota((CP, CP * RB), 0) == div(iota((CP, CP * RB), 1), RB))
    rw_rep = nn(rw_ref[...], spread).astype(BF16)
    right_all = nn(normed_rs, rw_rep)
    lane_r = mod(iota((SL, CP * RB), 1), RB)
    right_own = jnp.zeros((SL, CP * RB), F32)
    for q in range(RB):
        right_own = jnp.where(lane_r == q, right_all[q * SL : (q + 1) * SL], right_own)
    s_r[...] = right_own.astype(BF16)

    pl.semaphore_wait(barrier, N - 1)

    l_tile, l_slot = c // NKB, c % NKB
    blk = r * C + c
    r_tile, r_slot = blk // NB, blk % NB

    def left_copy(cc):
        return pltpu.make_async_remote_copy(
            src_ref=s_l,
            dst_ref=l3.at[s, pl.ds(l_slot * GPB, GPB)],
            send_sem=sl_sem.at[cc],
            recv_sem=rl_sem.at[l_slot * SQ + s],
            device_id=(r, cc, l_tile),
            device_id_type=MESH,
        )

    def right_copy(t):
        return pltpu.make_async_remote_copy(
            src_ref=s_r,
            dst_ref=r3.at[r_slot, s],
            send_sem=sr_sem.at[t],
            recv_sem=rr_sem.at[r_slot * SQ + s],
            device_id=(t // SQ, r_tile, t % SQ),
            device_id_type=MESH,
        )

    l_here = l_tile == s
    r_here = r_tile == c
    my_t = r * SQ + s
    for t in range(R * SQ):
        away = jnp.logical_not(jnp.logical_and(r_here, my_t == t))

        @pl.when(away)
        def _():
            right_copy(t).start()

    for cc in range(C):
        away = jnp.logical_not(jnp.logical_and(l_here, c == cc))

        @pl.when(away)
        def _():
            left_copy(cc).start()

    @pl.when(r_here)
    def _():
        r3[r_slot, s] = s_r[...]

    @pl.when(l_here)
    def _():
        l3[s, pl.ds(l_slot * GPB, GPB)] = s_l[...]

    wf[...] = wout_ref[...].astype(F32)
    for d in range(CP):
        w2[d * CP : (d + 1) * CP, :] = wf[pl.ds(d, CP, stride=CP), :].astype(BF16)
    cot = cot_ref[...]
    for dh in range(DH):
        part = nt(w2[dh * DG * CP : (dh + 1) * DG * CP, :], cot) * inverse
        part = part.astype(BF16)
        for d in range(DG):
            for g in range(G):
                og2[g * CP : (g + 1) * CP, dh * CH + d * IJ : dh * CH + (d + 1) * IJ] = part[
                    d * CP : (d + 1) * CP, g * IJ : (g + 1) * IJ
                ]
    fr, fc = iota((NB * PW, CH), 0), iota((NB * PW, CH), 1)
    fold = zero_one(
        fr == mod(div(fc, RB), NB) * PW + div(fc, IJ) * RB + mod(fc, RB)
    )
    i_lane = mod(div(iota((SL, CH), 1), cols), I4)

    for k in range(NKB):
        for sq in range(SQ):
            away = jnp.logical_not(jnp.logical_and(s == sq, c == s * NKB + k))

            @pl.when(away)
            def _():
                pltpu.make_async_remote_copy(
                    src_ref=s_l,
                    dst_ref=l3.at[sq, pl.ds(k * GPB, GPB)],
                    send_sem=sl_sem.at[0],
                    recv_sem=rl_sem.at[k * SQ + sq],
                    device_id=dev((me + 1) % N),
                    device_id_type=MESH,
                ).wait_recv()

    for b in range(NB):
        for sq in range(SQ):
            away = jnp.logical_not(jnp.logical_and(s == sq, blk == c * NB + b))

            @pl.when(away)
            def _():
                pltpu.make_async_remote_copy(
                    src_ref=s_r,
                    dst_ref=r3.at[b, sq],
                    send_sem=sr_sem.at[0],
                    recv_sem=rr_sem.at[b * SQ + sq],
                    device_id=dev((me + 1) % N),
                    device_id_type=MESH,
                ).wait_recv()

    left = jnp.concatenate([l3[sq].reshape(G * CP, LANES) for sq in range(SQ)], axis=1)
    for dh in range(DH):
        gathered = jnp.concatenate(
            [
                jnp.concatenate(
                    [r3[b, sq][:, dh * PW : (dh + 1) * PW] for b in range(NB)], axis=1
                )
                for sq in range(SQ)
            ],
            axis=0,
        )
        wide = nn(gathered, fold)
        for sq in range(SQ):
            for i in range(I4):
                start = (sq * I4 + i) * SL
                rbd[start : start + SL, dh * CH : (dh + 1) * CH] = jnp.where(
                    i_lane == i, wide[sq * SL : (sq + 1) * SL], 0.0
                ).astype(BF16)

    eye_k = zero_one(iota((KS, KS), 0) == iota((KS, KS), 1))
    left_turned = nt(eye_k, left).astype(BF16)
    folded = []
    for dh in range(DH):
        z = nn(left_turned, og2[:, dh * CH : (dh + 1) * CH])
        picked = []
        for sq in range(SQ):
            y = z[sq * I4 * SL : (sq * I4 + 1) * SL]
            for i in range(1, I4):
                start = (sq * I4 + i) * SL
                y = jnp.where(i_lane == i, z[start : start + SL], y)
            picked.append(y)
        folded.append(nt(jnp.concatenate(picked, axis=0).astype(BF16), fold))
    for b in range(NB):
        for sq in range(SQ):
            s_rg[b, sq] = jnp.concatenate(
                [f[sq * SL : (sq + 1) * SL, b * PW : (b + 1) * PW] for f in folded], axis=1
            ).astype(BF16)
            owner = c * NB + b
            here = jnp.logical_and(s == sq, blk == owner)

            @pl.when(jnp.logical_not(here))
            def _():
                pltpu.make_async_remote_copy(
                    src_ref=s_rg.at[b, sq],
                    dst_ref=r_rg.at[my_t],
                    send_sem=srg_sem.at[b * SQ + sq],
                    recv_sem=rrg_sem.at[my_t],
                    device_id=(owner // C, owner % C, sq),
                    device_id_type=MESH,
                ).start()

            @pl.when(here)
            def _():
                r_rg[my_t] = s_rg[b, sq]

    lg = nt(og2[...], rbd[...]).astype(BF16)
    for sq in range(SQ):
        for g in range(G):
            s_lg[sq, g] = lg[g * CP : (g + 1) * CP, sq * LANES : (sq + 1) * LANES]
    for k in range(NKB):
        for sq in range(SQ):
            here = jnp.logical_and(s == sq, c == s * NKB + k)

            @pl.when(jnp.logical_not(here))
            def _():
                pltpu.make_async_remote_copy(
                    src_ref=s_lg.at[sq, pl.ds(k * GPB, GPB)],
                    dst_ref=r_lg.at[c],
                    send_sem=slg_sem.at[k * SQ + sq],
                    recv_sem=rlg_sem.at[c],
                    device_id=(r, s * NKB + k, sq),
                    device_id_type=MESH,
                ).start()

            @pl.when(here)
            def _():
                r_lg[c] = s_lg[sq, pl.ds(k * GPB, GPB)]

    for dh in range(DH):
        part = nn(left, rbd[:, dh * CH : (dh + 1) * CH]) * inverse
        part = part.astype(BF16)
        for d in range(DG):
            for g in range(G):
                start = (dh * DG + d) * CP
                ot[start : start + CP, g * IJ : (g + 1) * IJ] = part[
                    g * CP : (g + 1) * CP, d * IJ : (d + 1) * IJ
                ]

    def scatter(src, dst, sems, pieces):
        stride = N // pieces
        mine = me // stride

        def one(target):
            p = target // stride
            pltpu.make_async_remote_copy(
                src_ref=src.at[p],
                dst_ref=dst.at[(me - target + N) % N - 1],
                send_sem=sems.at[0],
                recv_sem=sems.at[1],
                device_id=dev(target),
                device_id_type=MESH,
            ).start()

        def step(q, carry):
            one(((mine + q) % pieces) * stride)
            return carry

        lax.fori_loop(1, pieces, step, 0)
        if stride > 1:

            @pl.when(me % stride != 0)
            def _():
                one(mine * stride)

    def drain(ref, sem):
        pltpu.make_async_copy(ref, ref, sem).wait()

    def drain_pieces(ref, sem, pieces):
        stride = N // pieces
        if stride == 1:
            drain(ref.at[pl.ds(0, pieces - 1)], sem)
        else:

            @pl.when(me % stride == 0)
            def _():
                drain(ref.at[pl.ds(0, pieces - 1)], sem)

            @pl.when(me % stride != 0)
            def _():
                drain(ref, sem)

    def gather(src, dst, tot, sems, pieces, count):
        stride = N // pieces
        mine = me // stride

        def run():
            drain(dst, sems.at[1])
            total = src[mine].astype(F32)
            for k in range(N - 1):
                total = total + dst[k].astype(F32)
            tot[mine] = (total * (1.0 / count)).astype(tot.dtype)

            def step(k, carry):
                pltpu.make_async_remote_copy(
                    src_ref=tot.at[mine],
                    dst_ref=tot.at[mine],
                    send_sem=sems.at[2],
                    recv_sem=sems.at[3],
                    device_id=dev((me + k) % N),
                    device_id_type=MESH,
                ).start()
                return carry

            lax.fori_loop(1, N, step, 0)

        if stride == 1:
            run()
        else:
            pl.when(me % stride == 0)(run)

    def finish(src, dst, tot, sems, pieces):
        stride = N // pieces
        drain_pieces(tot, sems.at[3], pieces)
        drain_pieces(src, sems.at[0], pieces)
        if stride == 1:
            drain(dst, sems.at[2])
        else:

            @pl.when(me % stride == 0)
            def _():
                drain(dst, sems.at[2])

    pieces_w = s_w.shape[0]
    wo = nn(ot[...], cot).astype(s_w.dtype)
    s_w[...] = wo.reshape(s_w.shape)
    scatter(s_w, r_w, w_sem, pieces_w)

    for cc in range(C):
        here = jnp.logical_and(l_here, c == cc)

        @pl.when(jnp.logical_not(here))
        def _():
            pltpu.make_async_remote_copy(
                src_ref=s_l,
                dst_ref=r_lg.at[cc],
                send_sem=slg_sem.at[0],
                recv_sem=rlg_sem.at[cc],
                device_id=dev((me + 1) % N),
                device_id_type=MESH,
            ).wait_recv()

    for t in range(R * SQ):
        here = jnp.logical_and(r_here, my_t == t)

        @pl.when(jnp.logical_not(here))
        def _():
            pltpu.make_async_remote_copy(
                src_ref=s_r,
                dst_ref=r_rg.at[t],
                send_sem=srg_sem.at[0],
                recv_sem=rrg_sem.at[t],
                device_id=dev((me + 1) % N),
                device_id_type=MESH,
            ).wait_recv()

    gl = r_lg[0].astype(F32)
    for cc in range(1, C):
        gl = gl + r_lg[cc].astype(F32)
    gl = jnp.concatenate([gl[h] for h in range(GPB)], axis=1).astype(BF16)
    gr = r_rg[0].astype(F32)
    for t in range(1, R * SQ):
        gr = gr + r_rg[t].astype(F32)
    gr = gr.astype(BF16)
    repeat = zero_one(iota((M, SL), 1) == div(iota((M, SL), 0), RB))
    gr_rows = nn(repeat, gr)
    gr_rows = jnp.where(
        mod(iota((M, CP * RB), 0), RB) == mod(iota((M, CP * RB), 1), RB), gr_rows, 0.0
    ).astype(BF16)
    gr_t = nt(spread, gr_rows).astype(BF16)
    wg = jnp.concatenate([nn(gl, normed_rs), nn(gr_t, normed)], axis=0)
    pieces_v = s_v.shape[0]
    per_row = wg.shape[1] // LANES
    for p in range(pieces_v):
        u, v = p // per_row, p % per_row
        s_v[p] = wg[u * 8 : (u + 1) * 8, v * LANES : (v + 1) * LANES]
    scatter(s_v, r_v, v_sem, pieces_v)

    gather(s_w, r_w, g_w, w_sem, pieces_w, residues)

    back = zero_one(row_m == mod(col_m, SL) * RB + div(col_m, SL))
    gl_rows = nt(back, gl).astype(BF16)
    gr_cols = nt(gr_rows, spread).astype(BF16)
    ng = nt(gl_rows, lw_ref[...]) + nt(gr_cols, rw_ref[...])
    mean_grad = jnp.mean(ng, axis=1, keepdims=True)
    mean_cross = jnp.mean(ng * scaled, axis=1, keepdims=True)
    agrad_ref[...] = invstd * (ng - mean_grad - scaled * mean_cross)

    gather(s_v, r_v, g_v, v_sem, pieces_v, residues)

    eye_z = zero_one(iota((LANES, LANES), 0) == iota((LANES, LANES), 1))
    w2_t = nt(eye_z, w2[...]).astype(BF16)
    pair_t = nn(w2_t, ot[...])
    pair_ref[...] = (pair_t.T + bias_ref[...]).astype(BF16)

    finish(s_w, r_w, g_w, w_sem, pieces_w)
    flat = g_w[...].reshape(CP * CP, g_w.shape[2]).astype(F32)
    for d in range(CP):
        wog_ref[pl.ds(d, CP, stride=CP), :] = flat[d * CP : (d + 1) * CP, :]
    finish(s_v, r_v, g_v, v_sem, pieces_v)
    for p in range(pieces_v):
        u, v = p // per_row, p % per_row
        wg_ref[u * 8 : (u + 1) * 8, v * LANES : (v + 1) * LANES] = g_v[p]

    for t in range(R * SQ):
        away = jnp.logical_not(jnp.logical_and(r_here, my_t == t))

        @pl.when(away)
        def _():
            right_copy(t).wait_send()

    for cc in range(C):
        away = jnp.logical_not(jnp.logical_and(l_here, c == cc))

        @pl.when(away)
        def _():
            left_copy(cc).wait_send()

    for b in range(NB):
        for sq in range(SQ):
            here = jnp.logical_and(s == sq, blk == c * NB + b)

            @pl.when(jnp.logical_not(here))
            def _():
                pltpu.make_async_copy(
                    s_rg.at[b, sq], s_rg.at[b, sq], srg_sem.at[b * SQ + sq]
                ).wait()

    for k in range(NKB):
        for sq in range(SQ):
            here = jnp.logical_and(s == sq, c == s * NKB + k)

            @pl.when(jnp.logical_not(here))
            def _():
                part = s_lg.at[sq, pl.ds(k * GPB, GPB)]
                pltpu.make_async_copy(part, part, slg_sem.at[k * SQ + sq]).wait()


def body(alignment, left_weight, right_weight, out_weight, out_bias, cotangent):
    R, C, SQ = lax.axis_size("row"), lax.axis_size("col"), lax.axis_size("seq")
    N = R * C * SQ
    SL, RB, CM = alignment.shape
    CP = left_weight.shape[1]
    CZ = out_weight.shape[1]
    rows, cols = cotangent.shape[0], cotangent.shape[1]
    dims = (R, C, SQ, SL, RB, CP, rows, cols)
    I4 = LANES // SL
    GPB, G, NKB, NB = RB // I4, rows // I4, rows // RB, cols // RB
    IJ, KS = I4 * cols, SQ * I4 * SL
    piece = max(16, CP * CP // N)
    pieces_w = CP * CP // piece
    pieces_v = 2 * CP * CM // (8 * LANES)
    vmem = pl.BlockSpec(memory_space=pltpu.VMEM)
    dma = pltpu.SemaphoreType.DMA
    pair, agrad, wg, wog = pl.pallas_call(
        functools.partial(kernel, dims),
        out_shape=(
            jax.ShapeDtypeStruct((rows * cols, CZ), BF16),
            jax.ShapeDtypeStruct((SL * RB, CM), F32),
            jax.ShapeDtypeStruct((2 * CP, CM), F32),
            jax.ShapeDtypeStruct((CP * CP, CZ), F32),
        ),
        in_specs=[vmem] * 6,
        out_specs=(vmem,) * 4,
        scratch_shapes=[
            pltpu.VMEM((GPB, CP, LANES), BF16),
            pltpu.VMEM((SL, CP * RB), BF16),
            pltpu.VMEM((SQ, G, CP, LANES), BF16),
            pltpu.VMEM((NB, SQ, SL, CP * RB), BF16),
            pltpu.VMEM((KS, CP * IJ), BF16),
            pltpu.VMEM((G * CP, CP * IJ), BF16),
            pltpu.VMEM((CP * CP, rows * cols), BF16),
            pltpu.VMEM((CP * CP, CZ), F32),
            pltpu.VMEM((CP * CP, CZ), BF16),
            pltpu.VMEM((SQ, G, CP, LANES), BF16),
            pltpu.VMEM((NB, SQ, SL, CP * RB), BF16),
            pltpu.VMEM((C, GPB, CP, LANES), BF16),
            pltpu.VMEM((R * SQ, SL, CP * RB), BF16),
            pltpu.VMEM((pieces_w, piece, CZ), BF16),
            pltpu.VMEM((N - 1, piece, CZ), BF16),
            pltpu.VMEM((pieces_w, piece, CZ), BF16),
            pltpu.VMEM((pieces_v, 8, LANES), F32),
            pltpu.VMEM((N - 1, 8, LANES), F32),
            pltpu.VMEM((pieces_v, 8, LANES), F32),
            dma((C,)),
            dma((NKB * SQ,)),
            dma((R * SQ,)),
            dma((NB * SQ,)),
            dma((NKB * SQ,)),
            dma((C,)),
            dma((NB * SQ,)),
            dma((R * SQ,)),
            dma((4,)),
            dma((4,)),
        ],
        compiler_params=pltpu.CompilerParams(
            collective_id=0, has_side_effects=True, vmem_limit_bytes=56 * 1024 * 1024
        ),
        name="outer_product_mean",
    )(
        alignment.reshape(SL * RB, CM),
        left_weight,
        right_weight,
        out_weight,
        out_bias.reshape(1, CZ),
        cotangent.reshape(rows * cols, CZ),
    )
    return (
        pair.reshape(rows, cols, CZ),
        agrad.reshape(SL, RB, CM),
        wg[:CP].T,
        wg[CP:].T,
        wog,
    )


def solution(mesh):
    placed = (P("seq", ("row", "col"), None), P(), P(), P(), P(), P(("row", "seq"), "col", None))
    return jax.shard_map(
        body,
        mesh=mesh,
        in_specs=placed,
        out_specs=(P(("row", "seq"), "col", None), P("seq", ("row", "col"), None), P(), P(), P()),
        check_vma=False,
    )
```

```python
import functools

import jax
import jax.numpy as jnp
from jax import lax
from jax.experimental import pallas as pl
from jax.experimental.pallas import tpu as pltpu
from jax.sharding import PartitionSpec as P

F32 = jnp.float32
BF16 = jnp.bfloat16
MESH = pl.DeviceIdType.MESH
LANES = 128
DG = 8


def nn(a, b):
    return lax.dot_general(a, b, (((1,), (0,)), ((), ())), preferred_element_type=F32)


def nt(a, b):
    return lax.dot_general(a, b, (((1,), (1,)), ((), ())), preferred_element_type=F32)


def log2(n):
    assert n & (n - 1) == 0
    return n.bit_length() - 1


def div(x, n):
    return lax.shift_right_logical(x, jnp.int32(log2(n)))


def mod(x, n):
    return x & (n - 1)


def iota(shape, dim):
    return lax.broadcasted_iota(jnp.int32, shape, dim)


def zero_one(mask):
    return jnp.where(mask, 1.0, 0.0).astype(BF16)


def kernel(
    dims,
    align_ref,
    lw_ref,
    rw_ref,
    wout_hbm,
    bias_ref,
    cot_hbm,
    pair_hbm,
    agrad_hbm,
    gv_hbm,
    gw_hbm,
    wout_ref,
    cot_ref,
    pair_ref,
    agrad_ref,
    io_sem,
    s_l,
    s_r,
    l3,
    r3,
    rbd,
    og2,
    ot,
    wf,
    w2,
    s_lg,
    s_rg,
    r_lg,
    r_rg,
    s_w,
    r_w,
    g_w,
    s_v,
    r_v,
    g_v,
    sl_sem,
    rl_sem,
    sr_sem,
    rr_sem,
    slg_sem,
    rlg_sem,
    srg_sem,
    rrg_sem,
    w_sem,
    v_sem,
):
    R, C, SQ, SL, RB, CP, rows, cols = dims
    N = R * C * SQ
    I4 = LANES // SL
    GPB = RB // I4
    G = rows // I4
    NKB = rows // RB
    NB = cols // RB
    IJ = I4 * cols
    DH = CP // DG
    PW = DG * RB
    CH = DG * IJ
    KS = SQ * I4 * SL
    inverse = 1.0 / (SQ * SL)
    residues = RB * R * C

    r = lax.axis_index("row")
    c = lax.axis_index("col")
    s = lax.axis_index("seq")
    me = (r * C + c) * SQ + s

    def dev(lin):
        return (div(lin, C * SQ), mod(div(lin, SQ), C), mod(lin, SQ))

    loads = [
        pltpu.make_async_copy(wout_hbm, wout_ref, io_sem.at[0]),
        pltpu.make_async_copy(cot_hbm, cot_ref, io_sem.at[1]),
    ]
    for load in loads:
        load.start()
    stores = []

    def store(src, dst):
        stores.append(pltpu.make_async_copy(src, dst, io_sem.at[2 + len(stores)]))
        stores[-1].start()

    barrier = pltpu.get_barrier_semaphore()

    def greet(k, carry):
        pl.semaphore_signal(barrier, inc=1, device_id=dev(me ^ k), device_id_type=MESH)
        return carry

    lax.fori_loop(1, N, greet, 0)

    values = align_ref[...].astype(F32)
    center = values - jnp.mean(values, axis=1, keepdims=True)
    invstd = lax.rsqrt(jnp.mean(center * center, axis=1, keepdims=True) + 1e-05)
    scaled = center * invstd
    normed = scaled.astype(BF16)
    M = SL * RB
    row_m, col_m = iota((M, M), 0), iota((M, M), 1)
    perm = zero_one(col_m == mod(row_m, SL) * RB + div(row_m, SL))
    normed_rs = nn(perm, normed).astype(BF16)
    left_t = nt(lw_ref[...], normed_rs).astype(BF16)
    for h in range(GPB):
        s_l[h] = left_t[:, h * LANES : (h + 1) * LANES]
    spread = zero_one(iota((CP, CP * RB), 0) == div(iota((CP, CP * RB), 1), RB))
    CM = normed.shape[1]
    eye_m = zero_one(iota((CM, CM), 0) == iota((CM, CM), 1))
    rw_rep = nn(nt(eye_m, rw_ref[...]).astype(BF16), spread).astype(BF16)
    right_all = nn(normed_rs, rw_rep)
    lane_r = mod(iota((SL, CP * RB), 1), RB)
    right_own = jnp.zeros((SL, CP * RB), F32)
    for q in range(RB):
        right_own = jnp.where(lane_r == q, right_all[q * SL : (q + 1) * SL], right_own)
    s_r[...] = right_own.astype(BF16)

    pl.semaphore_wait(barrier, N - 1)

    l_tile, l_slot = c // NKB, c % NKB
    blk = r * C + c
    r_tile, r_slot = blk // NB, blk % NB

    def left_copy(cc):
        return pltpu.make_async_remote_copy(
            src_ref=s_l,
            dst_ref=l3.at[s, pl.ds(l_slot * GPB, GPB)],
            send_sem=sl_sem.at[cc],
            recv_sem=rl_sem.at[l_slot * SQ + s],
            device_id=(r, cc, l_tile),
            device_id_type=MESH,
        )

    def right_copy(t):
        return pltpu.make_async_remote_copy(
            src_ref=s_r,
            dst_ref=r3.at[r_slot, s],
            send_sem=sr_sem.at[t],
            recv_sem=rr_sem.at[r_slot * SQ + s],
            device_id=(t // SQ, r_tile, t % SQ),
            device_id_type=MESH,
        )

    l_here = l_tile == s
    r_here = r_tile == c
    my_t = r * SQ + s
    for t in range(R * SQ):
        away = jnp.logical_not(jnp.logical_and(r_here, my_t == t))

        @pl.when(away)
        def _():
            right_copy(t).start()

    for cc in range(C):
        away = jnp.logical_not(jnp.logical_and(l_here, c == cc))

        @pl.when(away)
        def _():
            left_copy(cc).start()

    @pl.when(r_here)
    def _():
        r3[r_slot, s] = s_r[...]

    @pl.when(l_here)
    def _():
        l3[s, pl.ds(l_slot * GPB, GPB)] = s_l[...]

    for load in loads:
        load.wait()
    wf[...] = wout_ref[...].astype(F32)
    for d in range(CP):
        w2[d * CP : (d + 1) * CP, :] = wf[pl.ds(d, CP, stride=CP), :].astype(BF16)
    cot = cot_ref[...]
    eye_z = zero_one(iota((LANES, LANES), 0) == iota((LANES, LANES), 1))
    w2_t = nt(eye_z, w2[...]).astype(BF16)
    for dh in range(DH):
        part = nt(w2[dh * DG * CP : (dh + 1) * DG * CP, :], cot) * inverse
        part = part.astype(BF16)
        for d in range(DG):
            for g in range(G):
                og2[g * CP : (g + 1) * CP, dh * CH + d * IJ : dh * CH + (d + 1) * IJ] = part[
                    d * CP : (d + 1) * CP, g * IJ : (g + 1) * IJ
                ]
    fr, fc = iota((NB * PW, CH), 0), iota((NB * PW, CH), 1)
    fold = zero_one(
        fr == mod(div(fc, RB), NB) * PW + div(fc, IJ) * RB + mod(fc, RB)
    )
    i_lane = mod(div(iota((SL, CH), 1), cols), I4)

    for k in range(NKB):
        for sq in range(SQ):
            away = jnp.logical_not(jnp.logical_and(s == sq, c == s * NKB + k))

            @pl.when(away)
            def _():
                pltpu.make_async_remote_copy(
                    src_ref=s_l,
                    dst_ref=l3.at[sq, pl.ds(k * GPB, GPB)],
                    send_sem=sl_sem.at[0],
                    recv_sem=rl_sem.at[k * SQ + sq],
                    device_id=dev(me ^ 1),
                    device_id_type=MESH,
                ).wait_recv()

    for b in range(NB):
        for sq in range(SQ):
            away = jnp.logical_not(jnp.logical_and(s == sq, blk == c * NB + b))

            @pl.when(away)
            def _():
                pltpu.make_async_remote_copy(
                    src_ref=s_r,
                    dst_ref=r3.at[b, sq],
                    send_sem=sr_sem.at[0],
                    recv_sem=rr_sem.at[b * SQ + sq],
                    device_id=dev(me ^ 1),
                    device_id_type=MESH,
                ).wait_recv()

    left = jnp.concatenate([l3[sq].reshape(G * CP, LANES) for sq in range(SQ)], axis=1)
    for dh in range(DH):
        gathered = jnp.concatenate(
            [
                jnp.concatenate(
                    [r3[b, sq][:, dh * PW : (dh + 1) * PW] for b in range(NB)], axis=1
                )
                for sq in range(SQ)
            ],
            axis=0,
        )
        wide = nn(gathered, fold)
        for sq in range(SQ):
            for i in range(I4):
                start = (sq * I4 + i) * SL
                rbd[start : start + SL, dh * CH : (dh + 1) * CH] = jnp.where(
                    i_lane == i, wide[sq * SL : (sq + 1) * SL], 0.0
                ).astype(BF16)

    for dh in range(DH):
        part = nn(left, rbd[:, dh * CH : (dh + 1) * CH]) * inverse
        part = part.astype(BF16)
        for d in range(DG):
            for g in range(G):
                start = (dh * DG + d) * CP
                ot[start : start + CP, g * IJ : (g + 1) * IJ] = part[
                    g * CP : (g + 1) * CP, d * IJ : (d + 1) * IJ
                ]

    def scatter(src, dst, sems, pieces):
        stride = N // pieces
        mine = div(me, stride)

        def one(target):
            p = div(target, stride)
            pltpu.make_async_remote_copy(
                src_ref=src.at[p],
                dst_ref=dst.at[(me ^ target) - 1],
                send_sem=sems.at[0],
                recv_sem=sems.at[1],
                device_id=dev(target),
                device_id_type=MESH,
            ).start()

        def step(q, carry):
            one((mine ^ q) * stride)
            return carry

        lax.fori_loop(1, pieces, step, 0)
        if stride > 1:

            @pl.when(mod(me, stride) != 0)
            def _():
                one(mine * stride)

    def drain(ref, sem):
        pltpu.make_async_copy(ref, ref, sem).wait()

    def drain_pieces(ref, sem, pieces):
        stride = N // pieces
        if stride == 1:
            drain(ref.at[pl.ds(0, pieces - 1)], sem)
        else:

            @pl.when(mod(me, stride) == 0)
            def _():
                drain(ref.at[pl.ds(0, pieces - 1)], sem)

            @pl.when(mod(me, stride) != 0)
            def _():
                drain(ref, sem)

    def gather(src, dst, tot, sems, pieces, count):
        stride = N // pieces
        mine = div(me, stride)

        def run():
            drain(dst, sems.at[1])
            total = src[mine].astype(F32)
            for k in range(N - 1):
                total = total + dst[k].astype(F32)
            tot[mine] = (total * (1.0 / count)).astype(tot.dtype)

            def step(k, carry):
                pltpu.make_async_remote_copy(
                    src_ref=tot.at[mine],
                    dst_ref=tot.at[mine],
                    send_sem=sems.at[2],
                    recv_sem=sems.at[3],
                    device_id=dev(me ^ k),
                    device_id_type=MESH,
                ).start()
                return carry

            lax.fori_loop(1, N, step, 0)

        if stride == 1:
            run()
        else:
            pl.when(mod(me, stride) == 0)(run)

    def finish(src, dst, tot, sems, pieces):
        stride = N // pieces
        drain_pieces(tot, sems.at[3], pieces)
        drain_pieces(src, sems.at[0], pieces)
        if stride == 1:
            drain(dst, sems.at[2])
        else:

            @pl.when(mod(me, stride) == 0)
            def _():
                drain(dst, sems.at[2])

    pieces_w = s_w.shape[0]
    wo = nn(ot[...], cot).astype(s_w.dtype)
    s_w[...] = wo.reshape(s_w.shape)
    scatter(s_w, r_w, w_sem, pieces_w)

    eye_k = zero_one(iota((KS, KS), 0) == iota((KS, KS), 1))
    left_turned = nt(eye_k, left).astype(BF16)
    folded = []
    for dh in range(DH):
        z = nn(left_turned, og2[:, dh * CH : (dh + 1) * CH])
        picked = []
        for sq in range(SQ):
            y = z[sq * I4 * SL : (sq * I4 + 1) * SL]
            for i in range(1, I4):
                start = (sq * I4 + i) * SL
                y = jnp.where(i_lane == i, z[start : start + SL], y)
            picked.append(y)
        folded.append(nt(jnp.concatenate(picked, axis=0).astype(BF16), fold))
    for b in range(NB):
        for sq in range(SQ):
            s_rg[b, sq] = jnp.concatenate(
                [f[sq * SL : (sq + 1) * SL, b * PW : (b + 1) * PW] for f in folded], axis=1
            ).astype(BF16)
            owner = c * NB + b
            here = jnp.logical_and(s == sq, blk == owner)

            @pl.when(jnp.logical_not(here))
            def _():
                pltpu.make_async_remote_copy(
                    src_ref=s_rg.at[b, sq],
                    dst_ref=r_rg.at[my_t],
                    send_sem=srg_sem.at[b * SQ + sq],
                    recv_sem=rrg_sem.at[my_t],
                    device_id=(owner // C, owner % C, sq),
                    device_id_type=MESH,
                ).start()

            @pl.when(here)
            def _():
                r_rg[my_t] = s_rg[b, sq]

    lg = nt(og2[...], rbd[...]).astype(BF16)
    for sq in range(SQ):
        for g in range(G):
            s_lg[sq, g] = lg[g * CP : (g + 1) * CP, sq * LANES : (sq + 1) * LANES]
    for k in range(NKB):
        for sq in range(SQ):
            here = jnp.logical_and(s == sq, c == s * NKB + k)

            @pl.when(jnp.logical_not(here))
            def _():
                pltpu.make_async_remote_copy(
                    src_ref=s_lg.at[sq, pl.ds(k * GPB, GPB)],
                    dst_ref=r_lg.at[c],
                    send_sem=slg_sem.at[k * SQ + sq],
                    recv_sem=rlg_sem.at[c],
                    device_id=(r, s * NKB + k, sq),
                    device_id_type=MESH,
                ).start()

            @pl.when(here)
            def _():
                r_lg[c] = s_lg[sq, pl.ds(k * GPB, GPB)]

    pair_t = nn(w2_t, ot[...])
    pair_ref[...] = (pair_t.T + bias_ref[...]).astype(BF16)
    store(pair_ref, pair_hbm)

    for cc in range(C):
        here = jnp.logical_and(l_here, c == cc)

        @pl.when(jnp.logical_not(here))
        def _():
            pltpu.make_async_remote_copy(
                src_ref=s_l,
                dst_ref=r_lg.at[cc],
                send_sem=slg_sem.at[0],
                recv_sem=rlg_sem.at[cc],
                device_id=dev(me ^ 1),
                device_id_type=MESH,
            ).wait_recv()

    for t in range(R * SQ):
        here = jnp.logical_and(r_here, my_t == t)

        @pl.when(jnp.logical_not(here))
        def _():
            pltpu.make_async_remote_copy(
                src_ref=s_r,
                dst_ref=r_rg.at[t],
                send_sem=srg_sem.at[0],
                recv_sem=rrg_sem.at[t],
                device_id=dev(me ^ 1),
                device_id_type=MESH,
            ).wait_recv()

    gl = r_lg[0].astype(F32)
    for cc in range(1, C):
        gl = gl + r_lg[cc].astype(F32)
    gl = jnp.concatenate([gl[h] for h in range(GPB)], axis=1).astype(BF16)
    gr = r_rg[0].astype(F32)
    for t in range(1, R * SQ):
        gr = gr + r_rg[t].astype(F32)
    gr = gr.astype(BF16)
    repeat = zero_one(iota((M, SL), 1) == div(iota((M, SL), 0), RB))
    gr_rows = nn(repeat, gr)
    gr_rows = jnp.where(
        mod(iota((M, CP * RB), 0), RB) == mod(iota((M, CP * RB), 1), RB), gr_rows, 0.0
    ).astype(BF16)
    gr_t = nt(spread, gr_rows).astype(BF16)
    wg = jnp.concatenate([nn(gl, normed_rs), nn(gr_t, normed)], axis=0)
    pieces_v = s_v.shape[0]
    per_row = wg.shape[1] // LANES
    for p in range(pieces_v):
        u, v = p // per_row, p % per_row
        s_v[p] = wg[u * 16 : (u + 1) * 16, v * LANES : (v + 1) * LANES].astype(s_v.dtype)
    scatter(s_v, r_v, v_sem, pieces_v)

    gather(s_w, r_w, g_w, w_sem, pieces_w, residues)

    back = zero_one(row_m == mod(col_m, SL) * RB + div(col_m, SL))
    gl_rows = nt(back, gl).astype(BF16)
    gr_cols = nt(gr_rows, spread).astype(BF16)
    ng = nn(gl_rows, lw_ref[...]) + nn(gr_cols, rw_ref[...])
    mean_grad = jnp.mean(ng, axis=1, keepdims=True)
    mean_cross = jnp.mean(ng * scaled, axis=1, keepdims=True)
    agrad_ref[...] = invstd * (ng - mean_grad - scaled * mean_cross)
    store(agrad_ref, agrad_hbm)

    gather(s_v, r_v, g_v, v_sem, pieces_v, residues)

    finish(s_v, r_v, g_v, v_sem, pieces_v)
    store(g_v, gv_hbm)
    finish(s_w, r_w, g_w, w_sem, pieces_w)
    store(g_w, gw_hbm)

    for t in range(R * SQ):
        away = jnp.logical_not(jnp.logical_and(r_here, my_t == t))

        @pl.when(away)
        def _():
            right_copy(t).wait_send()

    for cc in range(C):
        away = jnp.logical_not(jnp.logical_and(l_here, c == cc))

        @pl.when(away)
        def _():
            left_copy(cc).wait_send()

    for b in range(NB):
        for sq in range(SQ):
            here = jnp.logical_and(s == sq, blk == c * NB + b)

            @pl.when(jnp.logical_not(here))
            def _():
                pltpu.make_async_copy(
                    s_rg.at[b, sq], s_rg.at[b, sq], srg_sem.at[b * SQ + sq]
                ).wait()

    for k in range(NKB):
        for sq in range(SQ):
            here = jnp.logical_and(s == sq, c == s * NKB + k)

            @pl.when(jnp.logical_not(here))
            def _():
                part = s_lg.at[sq, pl.ds(k * GPB, GPB)]
                pltpu.make_async_copy(part, part, slg_sem.at[k * SQ + sq]).wait()

    for copy in stores:
        copy.wait()


def finishing(pair_in, agrad_in, gv_ref, gw_ref, pair_out, agrad_out, lwg, rwg, wog, sems):
    copies = [
        pltpu.make_async_copy(pair_in, pair_out, sems.at[0]),
        pltpu.make_async_copy(agrad_in, agrad_out, sems.at[1]),
    ]
    for copy in copies:
        copy.start()
    pieces, piece, CZ = gw_ref.shape
    CP = lwg.shape[0]
    flat = gw_ref[...].reshape(CP * CP, CZ).astype(F32)
    for d in range(CP):
        wog[pl.ds(d, CP, stride=CP), :] = flat[d * CP : (d + 1) * CP, :]
    per_row = lwg.shape[1] // LANES
    for p in range(gv_ref.shape[0]):
        u, v = p // per_row, p % per_row
        out, start = (lwg, u * 16) if u * 16 < CP else (rwg, u * 16 - CP)
        out[start : start + 16, v * LANES : (v + 1) * LANES] = gv_ref[p].astype(F32)
    for copy in copies:
        copy.wait()


def body(alignment, left_weight, right_weight, out_weight, out_bias, cotangent):
    R, C, SQ = lax.axis_size("row"), lax.axis_size("col"), lax.axis_size("seq")
    N = R * C * SQ
    SL, RB, CM = alignment.shape
    CP = left_weight.shape[1]
    CZ = out_weight.shape[1]
    rows, cols = cotangent.shape[0], cotangent.shape[1]
    dims = (R, C, SQ, SL, RB, CP, rows, cols)
    I4 = LANES // SL
    GPB, G, NKB, NB = RB // I4, rows // I4, rows // RB, cols // RB
    IJ, KS = I4 * cols, SQ * I4 * SL
    piece = max(16, CP * CP // N)
    pieces_w = CP * CP // piece
    pieces_v = 2 * CP * CM // (16 * LANES)
    vmem = pl.BlockSpec(memory_space=pltpu.VMEM)
    dma = pltpu.SemaphoreType.DMA
    hbm = pl.BlockSpec(memory_space=pl.ANY)
    pair, agrad, gv, gw = pl.pallas_call(
        functools.partial(kernel, dims),
        out_shape=(
            jax.ShapeDtypeStruct((rows * cols, CZ), BF16),
            jax.ShapeDtypeStruct((SL * RB, CM), F32),
            jax.ShapeDtypeStruct((pieces_v, 16, LANES), BF16),
            jax.ShapeDtypeStruct((pieces_w, piece, CZ), BF16),
        ),
        in_specs=[vmem, vmem, vmem, hbm, vmem, hbm],
        out_specs=(hbm,) * 4,
        scratch_shapes=[
            pltpu.VMEM((CP * CP, CZ), BF16),
            pltpu.VMEM((rows * cols, CZ), BF16),
            pltpu.VMEM((rows * cols, CZ), BF16),
            pltpu.VMEM((SL * RB, CM), F32),
            dma((6,)),
            pltpu.VMEM((GPB, CP, LANES), BF16),
            pltpu.VMEM((SL, CP * RB), BF16),
            pltpu.VMEM((SQ, G, CP, LANES), BF16),
            pltpu.VMEM((NB, SQ, SL, CP * RB), BF16),
            pltpu.VMEM((KS, CP * IJ), BF16),
            pltpu.VMEM((G * CP, CP * IJ), BF16),
            pltpu.VMEM((CP * CP, rows * cols), BF16),
            pltpu.VMEM((CP * CP, CZ), F32),
            pltpu.VMEM((CP * CP, CZ), BF16),
            pltpu.VMEM((SQ, G, CP, LANES), BF16),
            pltpu.VMEM((NB, SQ, SL, CP * RB), BF16),
            pltpu.VMEM((C, GPB, CP, LANES), BF16),
            pltpu.VMEM((R * SQ, SL, CP * RB), BF16),
            pltpu.VMEM((pieces_w, piece, CZ), BF16),
            pltpu.VMEM((N - 1, piece, CZ), BF16),
            pltpu.VMEM((pieces_w, piece, CZ), BF16),
            pltpu.VMEM((pieces_v, 16, LANES), BF16),
            pltpu.VMEM((N - 1, 16, LANES), BF16),
            pltpu.VMEM((pieces_v, 16, LANES), BF16),
            dma((C,)),
            dma((NKB * SQ,)),
            dma((R * SQ,)),
            dma((NB * SQ,)),
            dma((NKB * SQ,)),
            dma((C,)),
            dma((NB * SQ,)),
            dma((R * SQ,)),
            dma((4,)),
            dma((4,)),
        ],
        compiler_params=pltpu.CompilerParams(
            collective_id=0, has_side_effects=True, vmem_limit_bytes=56 * 1024 * 1024
        ),
        name="outer_product_mean",
    )(
        alignment.reshape(SL * RB, CM),
        left_weight.T,
        right_weight.T,
        out_weight,
        out_bias.reshape(1, CZ),
        cotangent.reshape(rows * cols, CZ),
    )
    pair, agrad, lwg, rwg, wog = pl.pallas_call(
        finishing,
        out_shape=(
            jax.ShapeDtypeStruct(pair.shape, BF16),
            jax.ShapeDtypeStruct(agrad.shape, F32),
            jax.ShapeDtypeStruct((CP, CM), F32),
            jax.ShapeDtypeStruct((CP, CM), F32),
            jax.ShapeDtypeStruct((CP * CP, CZ), F32),
        ),
        in_specs=[hbm, hbm, vmem, vmem],
        out_specs=(hbm, hbm, vmem, vmem, vmem),
        scratch_shapes=[dma((2,))],
        compiler_params=pltpu.CompilerParams(vmem_limit_bytes=56 * 1024 * 1024),
        name="finishing",
    )(pair, agrad, gv, gw)
    return (
        pair.reshape(rows, cols, CZ),
        agrad.reshape(SL, RB, CM),
        lwg.T,
        rwg.T,
        wog,
    )


def solution(mesh):
    placed = (P("seq", ("row", "col"), None), P(), P(), P(), P(), P(("row", "seq"), "col", None))
    return jax.shard_map(
        body,
        mesh=mesh,
        in_specs=placed,
        out_specs=(P(("row", "seq"), "col", None), P("seq", ("row", "col"), None), P(), P(), P()),
        check_vma=False,
    )
```

```python
import functools

import jax
import jax.numpy as jnp
from jax import lax
from jax.experimental import pallas as pl
from jax.experimental.pallas import tpu as pltpu
from jax.sharding import PartitionSpec as P

F32 = jnp.float32
BF16 = jnp.bfloat16
MESH = pl.DeviceIdType.MESH
LANES = 128
DG = 8


def nn(a, b):
    return lax.dot_general(a, b, (((1,), (0,)), ((), ())), preferred_element_type=F32)


def nt(a, b):
    return lax.dot_general(a, b, (((1,), (1,)), ((), ())), preferred_element_type=F32)


def log2(n):
    assert n & (n - 1) == 0
    return n.bit_length() - 1


def div(x, n):
    return lax.shift_right_logical(x, jnp.int32(log2(n)))


def mod(x, n):
    return x & (n - 1)


def iota(shape, dim):
    return lax.broadcasted_iota(jnp.int32, shape, dim)


def zero_one(mask):
    return jnp.where(mask, 1.0, 0.0).astype(BF16)


def kernel(
    dims,
    align_ref,
    lw_ref,
    rw_ref,
    wout_hbm,
    bias_ref,
    cot_hbm,
    pair_hbm,
    agrad_hbm,
    gv_hbm,
    gw_hbm,
    wout_ref,
    cot_ref,
    pair_ref,
    agrad_ref,
    io_sem,
    s_l,
    s_r,
    l3,
    r3,
    rbd,
    og2,
    ot,
    wf,
    w2,
    s_lg,
    s_rg,
    r_lg,
    r_rg,
    s_w,
    b_w,
    p_w,
    q_w,
    z_w,
    f_w,
    s_v,
    b_v,
    p_v,
    z_v,
    f_v,
    sl_sem,
    rl_sem,
    sr_sem,
    rr_sem,
    slg_sem,
    rlg_sem,
    srg_sem,
    rrg_sem,
    w_sem,
    v_sem,
):
    R, C, SQ, SL, RB, CP, rows, cols = dims
    N = R * C * SQ
    I4 = LANES // SL
    GPB = RB // I4
    G = rows // I4
    NKB = rows // RB
    NB = cols // RB
    IJ = I4 * cols
    DH = CP // DG
    PW = DG * RB
    CH = DG * IJ
    KS = SQ * I4 * SL
    inverse = 1.0 / (SQ * SL)
    residues = RB * R * C

    r = lax.axis_index("row")
    c = lax.axis_index("col")
    s = lax.axis_index("seq")
    me = (r * C + c) * SQ + s

    def dev(lin):
        return (div(lin, C * SQ), mod(div(lin, SQ), C), mod(lin, SQ))

    loads = [
        pltpu.make_async_copy(wout_hbm, wout_ref, io_sem.at[0]),
        pltpu.make_async_copy(cot_hbm, cot_ref, io_sem.at[1]),
    ]
    for load in loads:
        load.start()
    stores = []

    def store(src, dst):
        stores.append(pltpu.make_async_copy(src, dst, io_sem.at[2 + len(stores)]))
        stores[-1].start()

    barrier = pltpu.get_barrier_semaphore()

    def greet(k, carry):
        pl.semaphore_signal(barrier, inc=1, device_id=dev(me ^ k), device_id_type=MESH)
        return carry

    lax.fori_loop(1, N, greet, 0)

    values = align_ref[...].astype(F32)
    center = values - jnp.mean(values, axis=1, keepdims=True)
    invstd = lax.rsqrt(jnp.mean(center * center, axis=1, keepdims=True) + 1e-05)
    scaled = center * invstd
    normed = scaled.astype(BF16)
    M = SL * RB
    row_m, col_m = iota((M, M), 0), iota((M, M), 1)
    perm = zero_one(col_m == mod(row_m, SL) * RB + div(row_m, SL))
    normed_rs = nn(perm, normed).astype(BF16)
    left_t = nt(lw_ref[...], normed_rs).astype(BF16)
    for h in range(GPB):
        s_l[h] = left_t[:, h * LANES : (h + 1) * LANES]
    spread = zero_one(iota((CP, CP * RB), 0) == div(iota((CP, CP * RB), 1), RB))
    CM = normed.shape[1]
    eye_m = zero_one(iota((CM, CM), 0) == iota((CM, CM), 1))
    rw_rep = nn(nt(eye_m, rw_ref[...]).astype(BF16), spread).astype(BF16)
    right_all = nn(normed_rs, rw_rep)
    lane_r = mod(iota((SL, CP * RB), 1), RB)
    right_own = jnp.zeros((SL, CP * RB), F32)
    for q in range(RB):
        right_own = jnp.where(lane_r == q, right_all[q * SL : (q + 1) * SL], right_own)
    s_r[...] = right_own.astype(BF16)

    pl.semaphore_wait(barrier, N - 1)

    l_tile, l_slot = c // NKB, c % NKB
    blk = r * C + c
    r_tile, r_slot = blk // NB, blk % NB

    def left_copy(cc):
        return pltpu.make_async_remote_copy(
            src_ref=s_l,
            dst_ref=l3.at[s, pl.ds(l_slot * GPB, GPB)],
            send_sem=sl_sem.at[cc],
            recv_sem=rl_sem.at[l_slot * SQ + s],
            device_id=(r, cc, l_tile),
            device_id_type=MESH,
        )

    def right_copy(t):
        return pltpu.make_async_remote_copy(
            src_ref=s_r,
            dst_ref=r3.at[r_slot, s],
            send_sem=sr_sem.at[t],
            recv_sem=rr_sem.at[r_slot * SQ + s],
            device_id=(t // SQ, r_tile, t % SQ),
            device_id_type=MESH,
        )

    l_here = l_tile == s
    r_here = r_tile == c
    my_t = r * SQ + s
    for t in range(R * SQ):
        away = jnp.logical_not(jnp.logical_and(r_here, my_t == t))

        @pl.when(away)
        def _():
            right_copy(t).start()

    for cc in range(C):
        away = jnp.logical_not(jnp.logical_and(l_here, c == cc))

        @pl.when(away)
        def _():
            left_copy(cc).start()

    @pl.when(r_here)
    def _():
        r3[r_slot, s] = s_r[...]

    @pl.when(l_here)
    def _():
        l3[s, pl.ds(l_slot * GPB, GPB)] = s_l[...]

    for load in loads:
        load.wait()
    wf[...] = wout_ref[...].astype(F32)
    for d in range(CP):
        w2[d * CP : (d + 1) * CP, :] = wf[pl.ds(d, CP, stride=CP), :].astype(BF16)
    cot = cot_ref[...]
    eye_z = zero_one(iota((LANES, LANES), 0) == iota((LANES, LANES), 1))
    w2_t = nt(eye_z, w2[...]).astype(BF16)
    for dh in range(DH):
        part = nt(w2[dh * DG * CP : (dh + 1) * DG * CP, :], cot) * inverse
        part = part.astype(BF16)
        for d in range(DG):
            for g in range(G):
                og2[g * CP : (g + 1) * CP, dh * CH + d * IJ : dh * CH + (d + 1) * IJ] = part[
                    d * CP : (d + 1) * CP, g * IJ : (g + 1) * IJ
                ]
    fr, fc = iota((NB * PW, CH), 0), iota((NB * PW, CH), 1)
    fold = zero_one(
        fr == mod(div(fc, RB), NB) * PW + div(fc, IJ) * RB + mod(fc, RB)
    )
    i_lane = mod(div(iota((SL, CH), 1), cols), I4)

    for k in range(NKB):
        for sq in range(SQ):
            away = jnp.logical_not(jnp.logical_and(s == sq, c == s * NKB + k))

            @pl.when(away)
            def _():
                pltpu.make_async_remote_copy(
                    src_ref=s_l,
                    dst_ref=l3.at[sq, pl.ds(k * GPB, GPB)],
                    send_sem=sl_sem.at[0],
                    recv_sem=rl_sem.at[k * SQ + sq],
                    device_id=dev(me ^ 1),
                    device_id_type=MESH,
                ).wait_recv()

    for b in range(NB):
        for sq in range(SQ):
            away = jnp.logical_not(jnp.logical_and(s == sq, blk == c * NB + b))

            @pl.when(away)
            def _():
                pltpu.make_async_remote_copy(
                    src_ref=s_r,
                    dst_ref=r3.at[b, sq],
                    send_sem=sr_sem.at[0],
                    recv_sem=rr_sem.at[b * SQ + sq],
                    device_id=dev(me ^ 1),
                    device_id_type=MESH,
                ).wait_recv()

    left = jnp.concatenate([l3[sq].reshape(G * CP, LANES) for sq in range(SQ)], axis=1)
    for dh in range(DH):
        gathered = jnp.concatenate(
            [
                jnp.concatenate(
                    [r3[b, sq][:, dh * PW : (dh + 1) * PW] for b in range(NB)], axis=1
                )
                for sq in range(SQ)
            ],
            axis=0,
        )
        wide = nn(gathered, fold)
        for sq in range(SQ):
            for i in range(I4):
                start = (sq * I4 + i) * SL
                rbd[start : start + SL, dh * CH : (dh + 1) * CH] = jnp.where(
                    i_lane == i, wide[sq * SL : (sq + 1) * SL], 0.0
                ).astype(BF16)

    for dh in range(DH):
        part = nn(left, rbd[:, dh * CH : (dh + 1) * CH]) * inverse
        part = part.astype(BF16)
        for d in range(DG):
            for g in range(G):
                start = (dh * DG + d) * CP
                ot[start : start + CP, g * IJ : (g + 1) * IJ] = part[
                    g * CP : (g + 1) * CP, d * IJ : (d + 1) * IJ
                ]

    core = mod(r, 2)
    sibling = (r ^ 1, c, s)
    NZ = R * SQ // 2
    zq = div(r, 2) * SQ + s

    def send(src, dst, sems, phase, target):
        pltpu.make_async_remote_copy(
            src_ref=src,
            dst_ref=dst,
            send_sem=sems.at[2 * phase],
            recv_sem=sems.at[2 * phase + 1],
            device_id=target,
            device_id_type=MESH,
        ).start()

    def send_plane(src, dst, sems, phase):
        for k in range(1, C):
            send(src, dst, sems, phase, (r, c ^ k, s))

    def send_line(ref, sems, phase):
        for k in range(1, NZ):
            other = zq ^ k
            send(
                ref.at[zq],
                ref.at[zq],
                sems,
                phase,
                (div(other, SQ) * 2 + core, c, mod(other, SQ)),
            )

    def drain(ref, sem):
        pltpu.make_async_copy(ref, ref, sem).wait()

    def total(ref, count):
        out = ref[0].astype(F32)
        for k in range(1, count):
            out = out + ref[k].astype(F32)
        return out

    wo = nn(ot[...], cot)
    s_w[...] = wo.astype(BF16).reshape(s_w.shape)
    send(s_w.at[1 - core], b_w, w_sem, 0, sibling)

    eye_k = zero_one(iota((KS, KS), 0) == iota((KS, KS), 1))
    left_turned = nt(eye_k, left).astype(BF16)
    folded = []
    for dh in range(DH):
        z = nn(left_turned, og2[:, dh * CH : (dh + 1) * CH])
        picked = []
        for sq in range(SQ):
            y = z[sq * I4 * SL : (sq * I4 + 1) * SL]
            for i in range(1, I4):
                start = (sq * I4 + i) * SL
                y = jnp.where(i_lane == i, z[start : start + SL], y)
            picked.append(y)
        folded.append(nt(jnp.concatenate(picked, axis=0).astype(BF16), fold))
    for b in range(NB):
        for sq in range(SQ):
            s_rg[b, sq] = jnp.concatenate(
                [f[sq * SL : (sq + 1) * SL, b * PW : (b + 1) * PW] for f in folded], axis=1
            ).astype(BF16)
            owner = c * NB + b
            here = jnp.logical_and(s == sq, blk == owner)

            @pl.when(jnp.logical_not(here))
            def _():
                pltpu.make_async_remote_copy(
                    src_ref=s_rg.at[b, sq],
                    dst_ref=r_rg.at[my_t],
                    send_sem=srg_sem.at[b * SQ + sq],
                    recv_sem=rrg_sem.at[my_t],
                    device_id=(owner // C, owner % C, sq),
                    device_id_type=MESH,
                ).start()

            @pl.when(here)
            def _():
                r_rg[my_t] = s_rg[b, sq]

    drain(b_w, w_sem.at[1])
    p_w[...] = (s_w[core].astype(F32) + b_w[...].astype(F32)).astype(BF16).reshape(p_w.shape)
    for k in range(1, C):
        send(p_w.at[c ^ k], q_w.at[k - 1], w_sem, 1, (r, c ^ k, s))

    lg = nt(og2[...], rbd[...]).astype(BF16)
    for sq in range(SQ):
        for g in range(G):
            s_lg[sq, g] = lg[g * CP : (g + 1) * CP, sq * LANES : (sq + 1) * LANES]
    for k in range(NKB):
        for sq in range(SQ):
            here = jnp.logical_and(s == sq, c == s * NKB + k)

            @pl.when(jnp.logical_not(here))
            def _():
                pltpu.make_async_remote_copy(
                    src_ref=s_lg.at[sq, pl.ds(k * GPB, GPB)],
                    dst_ref=r_lg.at[c],
                    send_sem=slg_sem.at[k * SQ + sq],
                    recv_sem=rlg_sem.at[c],
                    device_id=(r, s * NKB + k, sq),
                    device_id_type=MESH,
                ).start()

            @pl.when(here)
            def _():
                r_lg[c] = s_lg[sq, pl.ds(k * GPB, GPB)]

    pair_t = nn(w2_t, ot[...])
    pair_ref[...] = (pair_t.T + bias_ref[...]).astype(BF16)
    store(pair_ref, pair_hbm)

    drain(q_w, w_sem.at[3])
    z_w[zq] = (p_w[c].astype(F32) + total(q_w, C - 1)).astype(BF16)
    send_line(z_w, w_sem, 2)

    for cc in range(C):
        here = jnp.logical_and(l_here, c == cc)

        @pl.when(jnp.logical_not(here))
        def _():
            pltpu.make_async_remote_copy(
                src_ref=s_l,
                dst_ref=r_lg.at[cc],
                send_sem=slg_sem.at[0],
                recv_sem=rlg_sem.at[cc],
                device_id=dev(me ^ 1),
                device_id_type=MESH,
            ).wait_recv()

    for t in range(R * SQ):
        here = jnp.logical_and(r_here, my_t == t)

        @pl.when(jnp.logical_not(here))
        def _():
            pltpu.make_async_remote_copy(
                src_ref=s_r,
                dst_ref=r_rg.at[t],
                send_sem=srg_sem.at[0],
                recv_sem=rrg_sem.at[t],
                device_id=dev(me ^ 1),
                device_id_type=MESH,
            ).wait_recv()

    gl = r_lg[0].astype(F32)
    for cc in range(1, C):
        gl = gl + r_lg[cc].astype(F32)
    gl = jnp.concatenate([gl[h] for h in range(GPB)], axis=1).astype(BF16)
    gr = r_rg[0].astype(F32)
    for t in range(1, R * SQ):
        gr = gr + r_rg[t].astype(F32)
    gr = gr.astype(BF16)
    repeat = zero_one(iota((M, SL), 1) == div(iota((M, SL), 0), RB))
    gr_rows = nn(repeat, gr)
    gr_rows = jnp.where(
        mod(iota((M, CP * RB), 0), RB) == mod(iota((M, CP * RB), 1), RB), gr_rows, 0.0
    ).astype(BF16)
    gr_t = nt(spread, gr_rows).astype(BF16)
    s_v[0] = nn(gl, normed_rs).astype(BF16)
    s_v[1] = nn(gr_t, normed).astype(BF16)
    send(s_v.at[1 - core], b_v, v_sem, 0, sibling)

    drain(z_w.at[pl.ds(0, NZ - 1)], w_sem.at[5])
    f_w[core, c] = (total(z_w, NZ) * (1.0 / residues)).astype(BF16)
    send_plane(f_w.at[core, c], f_w.at[core, c], w_sem, 3)

    drain(b_v, v_sem.at[1])
    p_v[c] = (s_v[core].astype(F32) + b_v[...].astype(F32)).astype(BF16)
    send_plane(p_v.at[c], p_v.at[c], v_sem, 1)

    back = zero_one(row_m == mod(col_m, SL) * RB + div(col_m, SL))
    gl_rows = nt(back, gl).astype(BF16)
    gr_cols = nt(gr_rows, spread).astype(BF16)
    ng = nn(gl_rows, lw_ref[...]) + nn(gr_cols, rw_ref[...])
    mean_grad = jnp.mean(ng, axis=1, keepdims=True)
    mean_cross = jnp.mean(ng * scaled, axis=1, keepdims=True)
    agrad_ref[...] = invstd * (ng - mean_grad - scaled * mean_cross)
    store(agrad_ref, agrad_hbm)

    drain(p_v.at[pl.ds(0, C - 1)], v_sem.at[3])
    z_v[zq] = total(p_v, C).astype(BF16)
    send_line(z_v, v_sem, 2)

    drain(f_w.at[0, pl.ds(0, C - 1)], w_sem.at[7])
    send(f_w.at[core], f_w.at[core], w_sem, 4, sibling)

    drain(z_v.at[pl.ds(0, NZ - 1)], v_sem.at[5])
    f_v[core] = (total(z_v, NZ) * (1.0 / residues)).astype(BF16)
    send(f_v.at[core], f_v.at[core], v_sem, 3, sibling)

    drain(f_w.at[0], w_sem.at[9])
    store(f_w, gw_hbm)
    drain(f_v.at[0], v_sem.at[7])
    store(f_v, gv_hbm)

    drain(b_w, w_sem.at[0])
    drain(q_w, w_sem.at[2])
    drain(z_w.at[pl.ds(0, NZ - 1)], w_sem.at[4])
    drain(f_w.at[0, pl.ds(0, C - 1)], w_sem.at[6])
    drain(f_w.at[0], w_sem.at[8])
    drain(b_v, v_sem.at[0])
    drain(p_v.at[pl.ds(0, C - 1)], v_sem.at[2])
    drain(z_v.at[pl.ds(0, NZ - 1)], v_sem.at[4])
    drain(f_v.at[0], v_sem.at[6])
    for t in range(R * SQ):
        away = jnp.logical_not(jnp.logical_and(r_here, my_t == t))

        @pl.when(away)
        def _():
            right_copy(t).wait_send()

    for cc in range(C):
        away = jnp.logical_not(jnp.logical_and(l_here, c == cc))

        @pl.when(away)
        def _():
            left_copy(cc).wait_send()

    for b in range(NB):
        for sq in range(SQ):
            here = jnp.logical_and(s == sq, blk == c * NB + b)

            @pl.when(jnp.logical_not(here))
            def _():
                pltpu.make_async_copy(
                    s_rg.at[b, sq], s_rg.at[b, sq], srg_sem.at[b * SQ + sq]
                ).wait()

    for k in range(NKB):
        for sq in range(SQ):
            here = jnp.logical_and(s == sq, c == s * NKB + k)

            @pl.when(jnp.logical_not(here))
            def _():
                part = s_lg.at[sq, pl.ds(k * GPB, GPB)]
                pltpu.make_async_copy(part, part, slg_sem.at[k * SQ + sq]).wait()

    for copy in stores:
        copy.wait()


def finishing(pair_in, agrad_in, gv_ref, gw_ref, pair_out, agrad_out, lwg, rwg, wog):
    pair_out[...] = pair_in[...]
    agrad_out[...] = agrad_in[...]
    CP = lwg.shape[0]
    flat = gw_ref[...].reshape(CP * CP, gw_ref.shape[-1]).astype(F32)
    for d in range(CP):
        wog[pl.ds(d, CP, stride=CP), :] = flat[d * CP : (d + 1) * CP, :]
    lwg[...] = gv_ref[0].astype(F32)
    rwg[...] = gv_ref[1].astype(F32)


def body(alignment, left_weight, right_weight, out_weight, out_bias, cotangent):
    R, C, SQ = lax.axis_size("row"), lax.axis_size("col"), lax.axis_size("seq")
    N = R * C * SQ
    SL, RB, CM = alignment.shape
    CP = left_weight.shape[1]
    CZ = out_weight.shape[1]
    rows, cols = cotangent.shape[0], cotangent.shape[1]
    dims = (R, C, SQ, SL, RB, CP, rows, cols)
    I4 = LANES // SL
    GPB, G, NKB, NB = RB // I4, rows // I4, rows // RB, cols // RB
    IJ, KS = I4 * cols, SQ * I4 * SL
    H, NZ = CP * CP // 2, R * SQ // 2
    vmem = pl.BlockSpec(memory_space=pltpu.VMEM)
    dma = pltpu.SemaphoreType.DMA
    hbm = pl.BlockSpec(memory_space=pl.ANY)
    pair, agrad, gv, gw = pl.pallas_call(
        functools.partial(kernel, dims),
        out_shape=(
            jax.ShapeDtypeStruct((rows * cols, CZ), BF16),
            jax.ShapeDtypeStruct((SL * RB, CM), F32),
            jax.ShapeDtypeStruct((2, CP, CM), BF16),
            jax.ShapeDtypeStruct((2, C, H // C, CZ), BF16),
        ),
        in_specs=[vmem, vmem, vmem, hbm, vmem, hbm],
        out_specs=(hbm,) * 4,
        scratch_shapes=[
            pltpu.VMEM((CP * CP, CZ), BF16),
            pltpu.VMEM((rows * cols, CZ), BF16),
            pltpu.VMEM((rows * cols, CZ), BF16),
            pltpu.VMEM((SL * RB, CM), F32),
            dma((6,)),
            pltpu.VMEM((GPB, CP, LANES), BF16),
            pltpu.VMEM((SL, CP * RB), BF16),
            pltpu.VMEM((SQ, G, CP, LANES), BF16),
            pltpu.VMEM((NB, SQ, SL, CP * RB), BF16),
            pltpu.VMEM((KS, CP * IJ), BF16),
            pltpu.VMEM((G * CP, CP * IJ), BF16),
            pltpu.VMEM((CP * CP, rows * cols), BF16),
            pltpu.VMEM((CP * CP, CZ), F32),
            pltpu.VMEM((CP * CP, CZ), BF16),
            pltpu.VMEM((SQ, G, CP, LANES), BF16),
            pltpu.VMEM((NB, SQ, SL, CP * RB), BF16),
            pltpu.VMEM((C, GPB, CP, LANES), BF16),
            pltpu.VMEM((R * SQ, SL, CP * RB), BF16),
            pltpu.VMEM((2, H, CZ), BF16),
            pltpu.VMEM((H, CZ), BF16),
            pltpu.VMEM((C, H // C, CZ), BF16),
            pltpu.VMEM((C - 1, H // C, CZ), BF16),
            pltpu.VMEM((NZ, H // C, CZ), BF16),
            pltpu.VMEM((2, C, H // C, CZ), BF16),
            pltpu.VMEM((2, CP, CM), BF16),
            pltpu.VMEM((CP, CM), BF16),
            pltpu.VMEM((C, CP, CM), BF16),
            pltpu.VMEM((NZ, CP, CM), BF16),
            pltpu.VMEM((2, CP, CM), BF16),
            dma((C,)),
            dma((NKB * SQ,)),
            dma((R * SQ,)),
            dma((NB * SQ,)),
            dma((NKB * SQ,)),
            dma((C,)),
            dma((NB * SQ,)),
            dma((R * SQ,)),
            dma((10,)),
            dma((8,)),
        ],
        compiler_params=pltpu.CompilerParams(
            collective_id=0, has_side_effects=True, vmem_limit_bytes=56 * 1024 * 1024
        ),
        name="outer_product_mean",
    )(
        alignment.reshape(SL * RB, CM),
        left_weight.T,
        right_weight.T,
        out_weight,
        out_bias.reshape(1, CZ),
        cotangent.reshape(rows * cols, CZ),
    )
    pair, agrad, lwg, rwg, wog = pl.pallas_call(
        finishing,
        out_shape=(
            jax.ShapeDtypeStruct(pair.shape, BF16),
            jax.ShapeDtypeStruct(agrad.shape, F32),
            jax.ShapeDtypeStruct((CP, CM), F32),
            jax.ShapeDtypeStruct((CP, CM), F32),
            jax.ShapeDtypeStruct((CP * CP, CZ), F32),
        ),
        in_specs=[vmem] * 4,
        out_specs=(vmem,) * 5,
        compiler_params=pltpu.CompilerParams(vmem_limit_bytes=56 * 1024 * 1024),
        name="finishing",
    )(pair, agrad, gv, gw)
    return (
        pair.reshape(rows, cols, CZ),
        agrad.reshape(SL, RB, CM),
        lwg.T,
        rwg.T,
        wog,
    )


def solution(mesh):
    placed = (P("seq", ("row", "col"), None), P(), P(), P(), P(), P(("row", "seq"), "col", None))
    return jax.shard_map(
        body,
        mesh=mesh,
        in_specs=placed,
        out_specs=(P(("row", "seq"), "col", None), P("seq", ("row", "col"), None), P(), P(), P()),
        check_vma=False,
    )
```

```python
import functools

import jax
import jax.numpy as jnp
from jax import lax
from jax.experimental import pallas as pl
from jax.experimental.pallas import tpu as pltpu
from jax.sharding import PartitionSpec as P

F32 = jnp.float32
BF16 = jnp.bfloat16
MESH = pl.DeviceIdType.MESH
LANES = 128
DG = 8


def nn(a, b):
    return lax.dot_general(a, b, (((1,), (0,)), ((), ())), preferred_element_type=F32)


def nt(a, b):
    return lax.dot_general(a, b, (((1,), (1,)), ((), ())), preferred_element_type=F32)


def log2(n):
    assert n & (n - 1) == 0
    return n.bit_length() - 1


def div(x, n):
    return lax.shift_right_logical(x, jnp.int32(log2(n)))


def mod(x, n):
    return x & (n - 1)


def iota(shape, dim):
    return lax.broadcasted_iota(jnp.int32, shape, dim)


def zero_one(mask):
    return jnp.where(mask, 1.0, 0.0).astype(BF16)


def kernel(
    dims,
    align_hbm,
    lw_hbm,
    rw_hbm,
    wout_hbm,
    bias_hbm,
    cot_hbm,
    pair_hbm,
    agrad_hbm,
    gv_hbm,
    gw_hbm,
    align_ref,
    lw_ref,
    rw_ref,
    wout_ref,
    bias_ref,
    cot_ref,
    pair_ref,
    agrad_ref,
    io_sem,
    s_l,
    s_r,
    l3,
    r3,
    rbd,
    og2,
    ot,
    wf,
    w2,
    s_lg,
    s_rg,
    r_lg,
    r_rg,
    s_w,
    b_w,
    p_w,
    q_w,
    z_w,
    f_w,
    s_v,
    b_v,
    p_v,
    z_v,
    f_v,
    sl_sem,
    rl_sem,
    sr_sem,
    rr_sem,
    slg_sem,
    rlg_sem,
    srg_sem,
    rrg_sem,
    w_sem,
    v_sem,
):
    R, C, SQ, SL, RB, CP, rows, cols = dims
    N = R * C * SQ
    I4 = LANES // SL
    GPB = RB // I4
    G = rows // I4
    NKB = rows // RB
    NB = cols // RB
    IJ = I4 * cols
    DH = CP // DG
    PW = DG * RB
    CH = DG * IJ
    KS = SQ * I4 * SL
    inverse = 1.0 / (SQ * SL)
    residues = RB * R * C

    r = lax.axis_index("row")
    c = lax.axis_index("col")
    s = lax.axis_index("seq")
    me = (r * C + c) * SQ + s

    def dev(lin):
        return (div(lin, C * SQ), mod(div(lin, SQ), C), mod(lin, SQ))

    loads = [
        pltpu.make_async_copy(src, dst, io_sem.at[k])
        for k, (src, dst) in enumerate(
            (
                (align_hbm, align_ref),
                (lw_hbm, lw_ref),
                (rw_hbm, rw_ref),
                (wout_hbm, wout_ref),
                (cot_hbm, cot_ref),
                (bias_hbm, bias_ref),
            )
        )
    ]
    for load in loads:
        load.start()
    stores = []

    def store(src, dst):
        stores.append(pltpu.make_async_copy(src, dst, io_sem.at[len(loads) + len(stores)]))
        stores[-1].start()

    barrier = pltpu.get_barrier_semaphore()

    def greet(k, carry):
        pl.semaphore_signal(barrier, inc=1, device_id=dev(me ^ k), device_id_type=MESH)
        return carry

    lax.fori_loop(1, N, greet, 0)

    for load in loads[:3]:
        load.wait()
    values = align_ref[...].astype(F32)
    center = values - jnp.mean(values, axis=1, keepdims=True)
    invstd = lax.rsqrt(jnp.mean(center * center, axis=1, keepdims=True) + 1e-05)
    scaled = center * invstd
    normed = scaled.astype(BF16)
    M = SL * RB
    row_m, col_m = iota((M, M), 0), iota((M, M), 1)
    perm = zero_one(col_m == mod(row_m, SL) * RB + div(row_m, SL))
    normed_rs = nn(perm, normed).astype(BF16)
    left_t = nt(lw_ref[...], normed_rs).astype(BF16)
    for h in range(GPB):
        s_l[h] = left_t[:, h * LANES : (h + 1) * LANES]
    spread = zero_one(iota((CP, CP * RB), 0) == div(iota((CP, CP * RB), 1), RB))
    CM = normed.shape[1]
    eye_m = zero_one(iota((CM, CM), 0) == iota((CM, CM), 1))
    rw_rep = nn(nt(eye_m, rw_ref[...]).astype(BF16), spread).astype(BF16)
    right_all = nn(normed_rs, rw_rep)
    lane_r = mod(iota((SL, CP * RB), 1), RB)
    right_own = jnp.zeros((SL, CP * RB), F32)
    for q in range(RB):
        right_own = jnp.where(lane_r == q, right_all[q * SL : (q + 1) * SL], right_own)
    s_r[...] = right_own.astype(BF16)

    pl.semaphore_wait(barrier, N - 1)

    l_tile, l_slot = c // NKB, c % NKB
    blk = r * C + c
    r_tile, r_slot = blk // NB, blk % NB

    def left_copy(cc):
        return pltpu.make_async_remote_copy(
            src_ref=s_l,
            dst_ref=l3.at[s, pl.ds(l_slot * GPB, GPB)],
            send_sem=sl_sem.at[cc],
            recv_sem=rl_sem.at[l_slot * SQ + s],
            device_id=(r, cc, l_tile),
            device_id_type=MESH,
        )

    def right_copy(t):
        return pltpu.make_async_remote_copy(
            src_ref=s_r,
            dst_ref=r3.at[r_slot, s],
            send_sem=sr_sem.at[t],
            recv_sem=rr_sem.at[r_slot * SQ + s],
            device_id=(t // SQ, r_tile, t % SQ),
            device_id_type=MESH,
        )

    l_here = l_tile == s
    r_here = r_tile == c
    my_t = r * SQ + s
    for t in range(R * SQ):
        away = jnp.logical_not(jnp.logical_and(r_here, my_t == t))

        @pl.when(away)
        def _():
            right_copy(t).start()

    for cc in range(C):
        away = jnp.logical_not(jnp.logical_and(l_here, c == cc))

        @pl.when(away)
        def _():
            left_copy(cc).start()

    @pl.when(r_here)
    def _():
        r3[r_slot, s] = s_r[...]

    @pl.when(l_here)
    def _():
        l3[s, pl.ds(l_slot * GPB, GPB)] = s_l[...]

    for load in loads[3:]:
        load.wait()
    wf[...] = wout_ref[...].astype(F32)
    for d in range(CP):
        w2[d * CP : (d + 1) * CP, :] = wf[pl.ds(d, CP, stride=CP), :].astype(BF16)
    cot = cot_ref[...]
    eye_z = zero_one(iota((LANES, LANES), 0) == iota((LANES, LANES), 1))
    w2_t = nt(eye_z, w2[...]).astype(BF16)
    for dh in range(DH):
        part = nt(w2[dh * DG * CP : (dh + 1) * DG * CP, :], cot) * inverse
        part = part.astype(BF16)
        for d in range(DG):
            for g in range(G):
                og2[g * CP : (g + 1) * CP, dh * CH + d * IJ : dh * CH + (d + 1) * IJ] = part[
                    d * CP : (d + 1) * CP, g * IJ : (g + 1) * IJ
                ]
    fr, fc = iota((NB * PW, CH), 0), iota((NB * PW, CH), 1)
    fold = zero_one(
        fr == mod(div(fc, RB), NB) * PW + div(fc, IJ) * RB + mod(fc, RB)
    )
    i_lane = mod(div(iota((SL, CH), 1), cols), I4)

    for k in range(NKB):
        for sq in range(SQ):
            away = jnp.logical_not(jnp.logical_and(s == sq, c == s * NKB + k))

            @pl.when(away)
            def _():
                pltpu.make_async_remote_copy(
                    src_ref=s_l,
                    dst_ref=l3.at[sq, pl.ds(k * GPB, GPB)],
                    send_sem=sl_sem.at[0],
                    recv_sem=rl_sem.at[k * SQ + sq],
                    device_id=dev(me ^ 1),
                    device_id_type=MESH,
                ).wait_recv()

    left = jnp.concatenate([l3[sq].reshape(G * CP, LANES) for sq in range(SQ)], axis=1)
    eye_k = zero_one(iota((KS, KS), 0) == iota((KS, KS), 1))
    left_turned = nt(eye_k, left).astype(BF16)
    folded = []
    for dh in range(DH):
        z = nn(left_turned, og2[:, dh * CH : (dh + 1) * CH])
        picked = []
        for sq in range(SQ):
            y = z[sq * I4 * SL : (sq * I4 + 1) * SL]
            for i in range(1, I4):
                start = (sq * I4 + i) * SL
                y = jnp.where(i_lane == i, z[start : start + SL], y)
            picked.append(y)
        folded.append(nt(jnp.concatenate(picked, axis=0).astype(BF16), fold))
    for b in range(NB):
        for sq in range(SQ):
            s_rg[b, sq] = jnp.concatenate(
                [f[sq * SL : (sq + 1) * SL, b * PW : (b + 1) * PW] for f in folded], axis=1
            ).astype(BF16)
            owner = c * NB + b
            here = jnp.logical_and(s == sq, blk == owner)

            @pl.when(jnp.logical_not(here))
            def _():
                pltpu.make_async_remote_copy(
                    src_ref=s_rg.at[b, sq],
                    dst_ref=r_rg.at[my_t],
                    send_sem=srg_sem.at[b * SQ + sq],
                    recv_sem=rrg_sem.at[my_t],
                    device_id=(owner // C, owner % C, sq),
                    device_id_type=MESH,
                ).start()

            @pl.when(here)
            def _():
                r_rg[my_t] = s_rg[b, sq]

    for b in range(NB):
        for sq in range(SQ):
            away = jnp.logical_not(jnp.logical_and(s == sq, blk == c * NB + b))

            @pl.when(away)
            def _():
                pltpu.make_async_remote_copy(
                    src_ref=s_r,
                    dst_ref=r3.at[b, sq],
                    send_sem=sr_sem.at[0],
                    recv_sem=rr_sem.at[b * SQ + sq],
                    device_id=dev(me ^ 1),
                    device_id_type=MESH,
                ).wait_recv()

    for dh in range(DH):
        gathered = jnp.concatenate(
            [
                jnp.concatenate(
                    [r3[b, sq][:, dh * PW : (dh + 1) * PW] for b in range(NB)], axis=1
                )
                for sq in range(SQ)
            ],
            axis=0,
        )
        wide = nn(gathered, fold)
        for sq in range(SQ):
            for i in range(I4):
                start = (sq * I4 + i) * SL
                rbd[start : start + SL, dh * CH : (dh + 1) * CH] = jnp.where(
                    i_lane == i, wide[sq * SL : (sq + 1) * SL], 0.0
                ).astype(BF16)

    lg = nt(og2[...], rbd[...]).astype(BF16)
    for sq in range(SQ):
        for g in range(G):
            s_lg[sq, g] = lg[g * CP : (g + 1) * CP, sq * LANES : (sq + 1) * LANES]
    for k in range(NKB):
        for sq in range(SQ):
            here = jnp.logical_and(s == sq, c == s * NKB + k)

            @pl.when(jnp.logical_not(here))
            def _():
                pltpu.make_async_remote_copy(
                    src_ref=s_lg.at[sq, pl.ds(k * GPB, GPB)],
                    dst_ref=r_lg.at[c],
                    send_sem=slg_sem.at[k * SQ + sq],
                    recv_sem=rlg_sem.at[c],
                    device_id=(r, s * NKB + k, sq),
                    device_id_type=MESH,
                ).start()

            @pl.when(here)
            def _():
                r_lg[c] = s_lg[sq, pl.ds(k * GPB, GPB)]

    for dh in range(DH):
        part = nn(left, rbd[:, dh * CH : (dh + 1) * CH]) * inverse
        part = part.astype(BF16)
        for d in range(DG):
            for g in range(G):
                start = (dh * DG + d) * CP
                ot[start : start + CP, g * IJ : (g + 1) * IJ] = part[
                    g * CP : (g + 1) * CP, d * IJ : (d + 1) * IJ
                ]

    core = mod(r, 2)
    sibling = (r ^ 1, c, s)
    NZ = R * SQ // 2
    zq = div(r, 2) * SQ + s

    def send(src, dst, sems, phase, target):
        pltpu.make_async_remote_copy(
            src_ref=src,
            dst_ref=dst,
            send_sem=sems.at[2 * phase],
            recv_sem=sems.at[2 * phase + 1],
            device_id=target,
            device_id_type=MESH,
        ).start()

    def send_plane(src, dst, sems, phase):
        for k in range(1, C):
            send(src, dst, sems, phase, (r, c ^ k, s))

    def send_line(ref, sems, phase):
        for k in range(1, NZ):
            other = zq ^ k
            send(
                ref.at[zq],
                ref.at[zq],
                sems,
                phase,
                (div(other, SQ) * 2 + core, c, mod(other, SQ)),
            )

    def drain(ref, sem):
        pltpu.make_async_copy(ref, ref, sem).wait()

    def total(ref, count):
        out = ref[0].astype(F32)
        for k in range(1, count):
            out = out + ref[k].astype(F32)
        return out

    wo = nn(ot[...], cot)
    s_w[...] = wo.astype(BF16).reshape(s_w.shape)
    send(s_w.at[1 - core], b_w, w_sem, 0, sibling)

    drain(b_w, w_sem.at[1])
    p_w[...] = (s_w[core].astype(F32) + b_w[...].astype(F32)).astype(BF16).reshape(p_w.shape)
    for k in range(1, C):
        send(p_w.at[c ^ k], q_w.at[k - 1], w_sem, 1, (r, c ^ k, s))

    for cc in range(C):
        here = jnp.logical_and(l_here, c == cc)

        @pl.when(jnp.logical_not(here))
        def _():
            pltpu.make_async_remote_copy(
                src_ref=s_l,
                dst_ref=r_lg.at[cc],
                send_sem=slg_sem.at[0],
                recv_sem=rlg_sem.at[cc],
                device_id=dev(me ^ 1),
                device_id_type=MESH,
            ).wait_recv()

    for t in range(R * SQ):
        here = jnp.logical_and(r_here, my_t == t)

        @pl.when(jnp.logical_not(here))
        def _():
            pltpu.make_async_remote_copy(
                src_ref=s_r,
                dst_ref=r_rg.at[t],
                send_sem=srg_sem.at[0],
                recv_sem=rrg_sem.at[t],
                device_id=dev(me ^ 1),
                device_id_type=MESH,
            ).wait_recv()

    gl = r_lg[0].astype(F32)
    for cc in range(1, C):
        gl = gl + r_lg[cc].astype(F32)
    gl = jnp.concatenate([gl[h] for h in range(GPB)], axis=1).astype(BF16)
    gr = r_rg[0].astype(F32)
    for t in range(1, R * SQ):
        gr = gr + r_rg[t].astype(F32)
    gr = gr.astype(BF16)
    repeat = zero_one(iota((M, SL), 1) == div(iota((M, SL), 0), RB))
    gr_rows = nn(repeat, gr)
    gr_rows = jnp.where(
        mod(iota((M, CP * RB), 0), RB) == mod(iota((M, CP * RB), 1), RB), gr_rows, 0.0
    ).astype(BF16)
    gr_t = nt(spread, gr_rows).astype(BF16)
    s_v[0] = nn(gl, normed_rs).astype(BF16)
    s_v[1] = nn(gr_t, normed).astype(BF16)
    send(s_v.at[1 - core], b_v, v_sem, 0, sibling)

    drain(q_w, w_sem.at[3])
    z_w[zq] = (p_w[c].astype(F32) + total(q_w, C - 1)).astype(BF16)
    send_line(z_w, w_sem, 2)

    drain(b_v, v_sem.at[1])
    p_v[c] = (s_v[core].astype(F32) + b_v[...].astype(F32)).astype(BF16)
    send_plane(p_v.at[c], p_v.at[c], v_sem, 1)

    back = zero_one(row_m == mod(col_m, SL) * RB + div(col_m, SL))
    gl_rows = nt(back, gl).astype(BF16)
    gr_cols = nt(gr_rows, spread).astype(BF16)
    ng = nn(gl_rows, lw_ref[...]) + nn(gr_cols, rw_ref[...])
    mean_grad = jnp.mean(ng, axis=1, keepdims=True)
    mean_cross = jnp.mean(ng * scaled, axis=1, keepdims=True)
    agrad_ref[...] = invstd * (ng - mean_grad - scaled * mean_cross)
    store(agrad_ref, agrad_hbm)

    drain(p_v.at[pl.ds(0, C - 1)], v_sem.at[3])
    z_v[zq] = total(p_v, C).astype(BF16)
    send_line(z_v, v_sem, 2)

    drain(z_w.at[pl.ds(0, NZ - 1)], w_sem.at[5])
    f_w[core, c] = (total(z_w, NZ) * (1.0 / residues)).astype(BF16)
    send_plane(f_w.at[core, c], f_w.at[core, c], w_sem, 3)

    pair_t = nn(w2_t, ot[...])
    pair_ref[...] = (pair_t.T + bias_ref[...]).astype(BF16)
    store(pair_ref, pair_hbm)

    drain(z_v.at[pl.ds(0, NZ - 1)], v_sem.at[5])
    f_v[core] = (total(z_v, NZ) * (1.0 / residues)).astype(BF16)
    send(f_v.at[core], f_v.at[core], v_sem, 3, sibling)

    drain(f_w.at[0, pl.ds(0, C - 1)], w_sem.at[7])
    send(f_w.at[core], f_w.at[core], w_sem, 4, sibling)

    drain(f_w.at[0], w_sem.at[9])
    store(f_w, gw_hbm)
    drain(f_v.at[0], v_sem.at[7])
    store(f_v, gv_hbm)

    drain(b_w, w_sem.at[0])
    drain(q_w, w_sem.at[2])
    drain(z_w.at[pl.ds(0, NZ - 1)], w_sem.at[4])
    drain(f_w.at[0, pl.ds(0, C - 1)], w_sem.at[6])
    drain(f_w.at[0], w_sem.at[8])
    drain(b_v, v_sem.at[0])
    drain(p_v.at[pl.ds(0, C - 1)], v_sem.at[2])
    drain(z_v.at[pl.ds(0, NZ - 1)], v_sem.at[4])
    drain(f_v.at[0], v_sem.at[6])
    for t in range(R * SQ):
        away = jnp.logical_not(jnp.logical_and(r_here, my_t == t))

        @pl.when(away)
        def _():
            right_copy(t).wait_send()

    for cc in range(C):
        away = jnp.logical_not(jnp.logical_and(l_here, c == cc))

        @pl.when(away)
        def _():
            left_copy(cc).wait_send()

    for b in range(NB):
        for sq in range(SQ):
            here = jnp.logical_and(s == sq, blk == c * NB + b)

            @pl.when(jnp.logical_not(here))
            def _():
                pltpu.make_async_copy(
                    s_rg.at[b, sq], s_rg.at[b, sq], srg_sem.at[b * SQ + sq]
                ).wait()

    for k in range(NKB):
        for sq in range(SQ):
            here = jnp.logical_and(s == sq, c == s * NKB + k)

            @pl.when(jnp.logical_not(here))
            def _():
                part = s_lg.at[sq, pl.ds(k * GPB, GPB)]
                pltpu.make_async_copy(part, part, slg_sem.at[k * SQ + sq]).wait()

    for copy in stores:
        copy.wait()


def finishing(pair_in, agrad_in, gv_ref, gw_ref, pair_out, agrad_out, lwg, rwg, wog):
    pair_out[...] = pair_in[...]
    agrad_out[...] = agrad_in[...]
    CP = lwg.shape[0]
    flat = gw_ref[...].reshape(CP * CP, gw_ref.shape[-1]).astype(F32)
    for d in range(CP):
        wog[pl.ds(d, CP, stride=CP), :] = flat[d * CP : (d + 1) * CP, :]
    lwg[...] = gv_ref[0].astype(F32)
    rwg[...] = gv_ref[1].astype(F32)


def body(alignment, left_weight, right_weight, out_weight, out_bias, cotangent):
    R, C, SQ = lax.axis_size("row"), lax.axis_size("col"), lax.axis_size("seq")
    N = R * C * SQ
    SL, RB, CM = alignment.shape
    CP = left_weight.shape[1]
    CZ = out_weight.shape[1]
    rows, cols = cotangent.shape[0], cotangent.shape[1]
    dims = (R, C, SQ, SL, RB, CP, rows, cols)
    I4 = LANES // SL
    GPB, G, NKB, NB = RB // I4, rows // I4, rows // RB, cols // RB
    IJ, KS = I4 * cols, SQ * I4 * SL
    H, NZ = CP * CP // 2, R * SQ // 2
    vmem = pl.BlockSpec(memory_space=pltpu.VMEM)
    dma = pltpu.SemaphoreType.DMA
    hbm = pl.BlockSpec(memory_space=pl.ANY)
    pair, agrad, gv, gw = pl.pallas_call(
        functools.partial(kernel, dims),
        out_shape=(
            jax.ShapeDtypeStruct((rows * cols, CZ), BF16),
            jax.ShapeDtypeStruct((SL * RB, CM), F32),
            jax.ShapeDtypeStruct((2, CP, CM), BF16),
            jax.ShapeDtypeStruct((2, C, H // C, CZ), BF16),
        ),
        in_specs=[hbm] * 6,
        out_specs=(hbm,) * 4,
        scratch_shapes=[
            pltpu.VMEM((SL * RB, CM), BF16),
            pltpu.VMEM((CP, CM), BF16),
            pltpu.VMEM((CP, CM), BF16),
            pltpu.VMEM((CP * CP, CZ), BF16),
            pltpu.VMEM((1, CZ), F32),
            pltpu.VMEM((rows * cols, CZ), BF16),
            pltpu.VMEM((rows * cols, CZ), BF16),
            pltpu.VMEM((SL * RB, CM), F32),
            dma((10,)),
            pltpu.VMEM((GPB, CP, LANES), BF16),
            pltpu.VMEM((SL, CP * RB), BF16),
            pltpu.VMEM((SQ, G, CP, LANES), BF16),
            pltpu.VMEM((NB, SQ, SL, CP * RB), BF16),
            pltpu.VMEM((KS, CP * IJ), BF16),
            pltpu.VMEM((G * CP, CP * IJ), BF16),
            pltpu.VMEM((CP * CP, rows * cols), BF16),
            pltpu.VMEM((CP * CP, CZ), F32),
            pltpu.VMEM((CP * CP, CZ), BF16),
            pltpu.VMEM((SQ, G, CP, LANES), BF16),
            pltpu.VMEM((NB, SQ, SL, CP * RB), BF16),
            pltpu.VMEM((C, GPB, CP, LANES), BF16),
            pltpu.VMEM((R * SQ, SL, CP * RB), BF16),
            pltpu.VMEM((2, H, CZ), BF16),
            pltpu.VMEM((H, CZ), BF16),
            pltpu.VMEM((C, H // C, CZ), BF16),
            pltpu.VMEM((C - 1, H // C, CZ), BF16),
            pltpu.VMEM((NZ, H // C, CZ), BF16),
            pltpu.VMEM((2, C, H // C, CZ), BF16),
            pltpu.VMEM((2, CP, CM), BF16),
            pltpu.VMEM((CP, CM), BF16),
            pltpu.VMEM((C, CP, CM), BF16),
            pltpu.VMEM((NZ, CP, CM), BF16),
            pltpu.VMEM((2, CP, CM), BF16),
            dma((C,)),
            dma((NKB * SQ,)),
            dma((R * SQ,)),
            dma((NB * SQ,)),
            dma((NKB * SQ,)),
            dma((C,)),
            dma((NB * SQ,)),
            dma((R * SQ,)),
            dma((10,)),
            dma((8,)),
        ],
        compiler_params=pltpu.CompilerParams(
            collective_id=0, has_side_effects=True, vmem_limit_bytes=56 * 1024 * 1024
        ),
        name="outer_product_mean",
    )(
        alignment.reshape(SL * RB, CM),
        left_weight.T,
        right_weight.T,
        out_weight,
        out_bias.reshape(1, CZ),
        cotangent.reshape(rows * cols, CZ),
    )
    pair, agrad, lwg, rwg, wog = pl.pallas_call(
        finishing,
        out_shape=(
            jax.ShapeDtypeStruct(pair.shape, BF16),
            jax.ShapeDtypeStruct(agrad.shape, F32),
            jax.ShapeDtypeStruct((CP, CM), F32),
            jax.ShapeDtypeStruct((CP, CM), F32),
            jax.ShapeDtypeStruct((CP * CP, CZ), F32),
        ),
        in_specs=[vmem] * 4,
        out_specs=(vmem,) * 5,
        compiler_params=pltpu.CompilerParams(vmem_limit_bytes=56 * 1024 * 1024),
        name="finishing",
    )(pair, agrad, gv, gw)
    return (
        pair.reshape(rows, cols, CZ),
        agrad.reshape(SL, RB, CM),
        lwg.T,
        rwg.T,
        wog,
    )


def solution(mesh):
    placed = (P("seq", ("row", "col"), None), P(), P(), P(), P(), P(("row", "seq"), "col", None))
    return jax.shard_map(
        body,
        mesh=mesh,
        in_specs=placed,
        out_specs=(P(("row", "seq"), "col", None), P("seq", ("row", "col"), None), P(), P(), P()),
        check_vma=False,
    )
```

```python
import functools

import jax
import jax.numpy as jnp
from jax import lax
from jax.experimental import pallas as pl
from jax.experimental.pallas import tpu as pltpu
from jax.sharding import PartitionSpec as P

F32 = jnp.float32
BF16 = jnp.bfloat16
MESH = pl.DeviceIdType.MESH
LANES = 128
DG = 8


def nn(a, b):
    return lax.dot_general(a, b, (((1,), (0,)), ((), ())), preferred_element_type=F32)


def nt(a, b):
    return lax.dot_general(a, b, (((1,), (1,)), ((), ())), preferred_element_type=F32)


def log2(n):
    assert n & (n - 1) == 0
    return n.bit_length() - 1


def div(x, n):
    return lax.shift_right_logical(x, jnp.int32(log2(n)))


def mod(x, n):
    return x & (n - 1)


def iota(shape, dim):
    return lax.broadcasted_iota(jnp.int32, shape, dim)


def zero_one(mask):
    return jnp.where(mask, 1.0, 0.0).astype(BF16)


def kernel(
    dims,
    align_hbm,
    lw_hbm,
    rw_hbm,
    wout_hbm,
    bias_hbm,
    cot_hbm,
    pair_hbm,
    agrad_hbm,
    gv_hbm,
    gw_hbm,
    align_ref,
    lw_ref,
    rw_ref,
    wout_ref,
    bias_ref,
    cot_ref,
    pair_ref,
    agrad_ref,
    io_sem,
    s_l,
    s_r,
    l3,
    r3,
    rbd,
    og2,
    ot,
    wf,
    w2,
    s_lg,
    s_rg,
    r_lg,
    r_rg,
    s_w,
    b_w,
    p_w,
    q_w,
    z_w,
    f_w,
    s_v,
    b_v,
    p_v,
    z_v,
    f_v,
    sl_sem,
    rl_sem,
    sr_sem,
    rr_sem,
    slg_sem,
    rlg_sem,
    srg_sem,
    rrg_sem,
    fw_sem,
    w_sem,
    v_sem,
):
    R, C, SQ, SL, RB, CP, rows, cols = dims
    N = R * C * SQ
    I4 = LANES // SL
    GPB = RB // I4
    G = rows // I4
    NKB = rows // RB
    NB = cols // RB
    IJ = I4 * cols
    DH = CP // DG
    PW = DG * RB
    CH = DG * IJ
    KS = SQ * I4 * SL
    inverse = 1.0 / (SQ * SL)
    residues = RB * R * C

    r = lax.axis_index("row")
    c = lax.axis_index("col")
    s = lax.axis_index("seq")
    me = (r * C + c) * SQ + s
    core = mod(r, 2)
    sibling = (r ^ 1, c, s)

    def dev(lin):
        return (div(lin, C * SQ), mod(div(lin, SQ), C), mod(lin, SQ))

    loads = [
        pltpu.make_async_copy(src, dst, io_sem.at[k])
        for k, (src, dst) in enumerate(
            (
                (align_hbm, align_ref),
                (lw_hbm, lw_ref),
                (rw_hbm, rw_ref),
                (wout_hbm, wout_ref),
                (cot_hbm, cot_ref),
                (bias_hbm, bias_ref),
            )
        )
    ]
    for load in loads:
        load.start()
    stores = []

    def store(src, dst):
        stores.append(pltpu.make_async_copy(src, dst, io_sem.at[len(loads) + len(stores)]))
        stores[-1].start()

    barrier = pltpu.get_barrier_semaphore()

    def greet(k, carry):
        pl.semaphore_signal(barrier, inc=1, device_id=dev(me ^ k), device_id_type=MESH)
        return carry

    lax.fori_loop(1, N, greet, 0)

    for load in loads[:3]:
        load.wait()
    values = align_ref[...].astype(F32)
    center = values - jnp.mean(values, axis=1, keepdims=True)
    invstd = lax.rsqrt(jnp.mean(center * center, axis=1, keepdims=True) + 1e-05)
    scaled = center * invstd
    normed = scaled.astype(BF16)
    M = SL * RB
    row_m, col_m = iota((M, M), 0), iota((M, M), 1)
    perm = zero_one(col_m == mod(row_m, SL) * RB + div(row_m, SL))
    normed_rs = nn(perm, normed).astype(BF16)
    left_t = nt(lw_ref[...], normed_rs).astype(BF16)
    for h in range(GPB):
        s_l[h] = left_t[:, h * LANES : (h + 1) * LANES]
    spread = zero_one(iota((CP, CP * RB), 0) == div(iota((CP, CP * RB), 1), RB))
    CM = normed.shape[1]
    eye_m = zero_one(iota((CM, CM), 0) == iota((CM, CM), 1))
    rw_rep = nn(nt(eye_m, rw_ref[...]).astype(BF16), spread).astype(BF16)
    right_all = nn(normed_rs, rw_rep)
    lane_r = mod(iota((SL, CP * RB), 1), RB)
    right_own = jnp.zeros((SL, CP * RB), F32)
    for q in range(RB):
        right_own = jnp.where(lane_r == q, right_all[q * SL : (q + 1) * SL], right_own)
    s_r[...] = right_own.astype(BF16)

    pl.semaphore_wait(barrier, N - 1)

    l_tile, l_slot = c // NKB, c % NKB
    blk = r * C + c
    r_tile, r_slot = blk // NB, blk % NB

    def left_copy(cc):
        return pltpu.make_async_remote_copy(
            src_ref=s_l,
            dst_ref=l3.at[s, pl.ds(l_slot * GPB, GPB)],
            send_sem=sl_sem.at[cc],
            recv_sem=rl_sem.at[l_slot * SQ + s],
            device_id=(r, cc, l_tile),
            device_id_type=MESH,
        )

    def right_copy(t):
        return pltpu.make_async_remote_copy(
            src_ref=s_r,
            dst_ref=r3.at[r_slot, s],
            send_sem=sr_sem.at[t],
            recv_sem=rr_sem.at[r_slot * SQ + s],
            device_id=(t // SQ, r_tile, t % SQ),
            device_id_type=MESH,
        )

    l_here = l_tile == s
    r_here = r_tile == c
    my_t = r * SQ + s
    for t in range(R * SQ):
        away = jnp.logical_not(jnp.logical_and(r_here, my_t == t))
        away = jnp.logical_and(away, mod(r_slot, 2) == (t // SQ) % 2)

        @pl.when(away)
        def _():
            right_copy(t).start()

    for cc in range(C):
        away = jnp.logical_not(jnp.logical_and(l_here, c == cc))

        @pl.when(away)
        def _():
            left_copy(cc).start()

    @pl.when(r_here)
    def _():
        r3[r_slot, s] = s_r[...]

    @pl.when(l_here)
    def _():
        l3[s, pl.ds(l_slot * GPB, GPB)] = s_l[...]

    for load in loads[3:]:
        load.wait()
    wf[...] = wout_ref[...].astype(F32)
    for d in range(CP):
        w2[d * CP : (d + 1) * CP, :] = wf[pl.ds(d, CP, stride=CP), :].astype(BF16)
    cot = cot_ref[...]
    eye_z = zero_one(iota((LANES, LANES), 0) == iota((LANES, LANES), 1))
    w2_t = nt(eye_z, w2[...]).astype(BF16)
    for dh in range(DH):
        part = nt(w2[dh * DG * CP : (dh + 1) * DG * CP, :], cot) * inverse
        part = part.astype(BF16)
        for d in range(DG):
            for g in range(G):
                og2[g * CP : (g + 1) * CP, dh * CH + d * IJ : dh * CH + (d + 1) * IJ] = part[
                    d * CP : (d + 1) * CP, g * IJ : (g + 1) * IJ
                ]
    fr, fc = iota((NB * PW, CH), 0), iota((NB * PW, CH), 1)
    fold = zero_one(
        fr == mod(div(fc, RB), NB) * PW + div(fc, IJ) * RB + mod(fc, RB)
    )
    i_lane = mod(div(iota((SL, CH), 1), cols), I4)

    for k in range(NKB):
        for sq in range(SQ):
            away = jnp.logical_not(jnp.logical_and(s == sq, c == s * NKB + k))

            @pl.when(away)
            def _():
                pltpu.make_async_remote_copy(
                    src_ref=s_l,
                    dst_ref=l3.at[sq, pl.ds(k * GPB, GPB)],
                    send_sem=sl_sem.at[0],
                    recv_sem=rl_sem.at[k * SQ + sq],
                    device_id=dev(me ^ 1),
                    device_id_type=MESH,
                ).wait_recv()

    def hand_over(b, sq):
        return pltpu.make_async_remote_copy(
            src_ref=r3.at[b, sq],
            dst_ref=r3.at[b, sq],
            send_sem=fw_sem.at[b * SQ + sq],
            recv_sem=rr_sem.at[b * SQ + sq],
            device_id=sibling,
            device_id_type=MESH,
        )

    def from_sibling(b, sq):
        return jnp.logical_and(s == sq, (r ^ 1) * C + c == c * NB + b)

    def await_right(first):
        for b in range(NB):
            for sq in range(SQ):
                mine = core == b % 2
                if not first:
                    mine = jnp.logical_not(mine)
                own = jnp.logical_and(s == sq, blk == c * NB + b)

                @pl.when(jnp.logical_and(mine, jnp.logical_not(own)))
                def _():
                    hand_over(b, sq).wait_recv()

                if first:

                    @pl.when(jnp.logical_and(mine, jnp.logical_not(from_sibling(b, sq))))
                    def _():
                        hand_over(b, sq).start()

    await_right(True)

    left = jnp.concatenate([l3[sq].reshape(G * CP, LANES) for sq in range(SQ)], axis=1)
    eye_k = zero_one(iota((KS, KS), 0) == iota((KS, KS), 1))
    left_turned = nt(eye_k, left).astype(BF16)
    folded = []
    for dh in range(DH):
        z = nn(left_turned, og2[:, dh * CH : (dh + 1) * CH])
        picked = []
        for sq in range(SQ):
            y = z[sq * I4 * SL : (sq * I4 + 1) * SL]
            for i in range(1, I4):
                start = (sq * I4 + i) * SL
                y = jnp.where(i_lane == i, z[start : start + SL], y)
            picked.append(y)
        folded.append(nt(jnp.concatenate(picked, axis=0).astype(BF16), fold))
    for b in range(NB):
        for sq in range(SQ):
            s_rg[b, sq] = jnp.concatenate(
                [f[sq * SL : (sq + 1) * SL, b * PW : (b + 1) * PW] for f in folded], axis=1
            ).astype(BF16)
            owner = c * NB + b
            here = jnp.logical_and(s == sq, blk == owner)

            @pl.when(jnp.logical_not(here))
            def _():
                pltpu.make_async_remote_copy(
                    src_ref=s_rg.at[b, sq],
                    dst_ref=r_rg.at[my_t],
                    send_sem=srg_sem.at[b * SQ + sq],
                    recv_sem=rrg_sem.at[my_t],
                    device_id=(owner // C, owner % C, sq),
                    device_id_type=MESH,
                ).start()

            @pl.when(here)
            def _():
                r_rg[my_t] = s_rg[b, sq]

    await_right(False)

    for dh in range(DH):
        gathered = jnp.concatenate(
            [
                jnp.concatenate(
                    [r3[b, sq][:, dh * PW : (dh + 1) * PW] for b in range(NB)], axis=1
                )
                for sq in range(SQ)
            ],
            axis=0,
        )
        wide = nn(gathered, fold)
        for sq in range(SQ):
            for i in range(I4):
                start = (sq * I4 + i) * SL
                rbd[start : start + SL, dh * CH : (dh + 1) * CH] = jnp.where(
                    i_lane == i, wide[sq * SL : (sq + 1) * SL], 0.0
                ).astype(BF16)

    lg = nt(og2[...], rbd[...]).astype(BF16)
    for sq in range(SQ):
        for g in range(G):
            s_lg[sq, g] = lg[g * CP : (g + 1) * CP, sq * LANES : (sq + 1) * LANES]
    for k in range(NKB):
        for sq in range(SQ):
            here = jnp.logical_and(s == sq, c == s * NKB + k)

            @pl.when(jnp.logical_not(here))
            def _():
                pltpu.make_async_remote_copy(
                    src_ref=s_lg.at[sq, pl.ds(k * GPB, GPB)],
                    dst_ref=r_lg.at[c],
                    send_sem=slg_sem.at[k * SQ + sq],
                    recv_sem=rlg_sem.at[c],
                    device_id=(r, s * NKB + k, sq),
                    device_id_type=MESH,
                ).start()

            @pl.when(here)
            def _():
                r_lg[c] = s_lg[sq, pl.ds(k * GPB, GPB)]

    for dh in range(DH):
        part = nn(left, rbd[:, dh * CH : (dh + 1) * CH]) * inverse
        part = part.astype(BF16)
        for d in range(DG):
            for g in range(G):
                start = (dh * DG + d) * CP
                ot[start : start + CP, g * IJ : (g + 1) * IJ] = part[
                    g * CP : (g + 1) * CP, d * IJ : (d + 1) * IJ
                ]

    NZ = R * SQ // 2
    zq = div(r, 2) * SQ + s

    def send(src, dst, sems, phase, target):
        pltpu.make_async_remote_copy(
            src_ref=src,
            dst_ref=dst,
            send_sem=sems.at[2 * phase],
            recv_sem=sems.at[2 * phase + 1],
            device_id=target,
            device_id_type=MESH,
        ).start()

    def send_plane(src, dst, sems, phase):
        for k in range(1, C):
            send(src, dst, sems, phase, (r, c ^ k, s))

    def send_line(ref, sems, phase):
        for k in range(1, NZ):
            other = zq ^ k
            send(
                ref.at[zq],
                ref.at[zq],
                sems,
                phase,
                (div(other, SQ) * 2 + core, c, mod(other, SQ)),
            )

    def drain(ref, sem):
        pltpu.make_async_copy(ref, ref, sem).wait()

    def total(ref, count):
        out = ref[0].astype(F32)
        for k in range(1, count):
            out = out + ref[k].astype(F32)
        return out

    wo = nn(ot[...], cot)
    s_w[...] = wo.astype(BF16).reshape(s_w.shape)
    send(s_w.at[1 - core], b_w, w_sem, 0, sibling)

    drain(b_w, w_sem.at[1])
    p_w[...] = (s_w[core].astype(F32) + b_w[...].astype(F32)).astype(BF16).reshape(p_w.shape)
    for k in range(1, C):
        send(p_w.at[c ^ k], q_w.at[k - 1], w_sem, 1, (r, c ^ k, s))

    for cc in range(C):
        here = jnp.logical_and(l_here, c == cc)

        @pl.when(jnp.logical_not(here))
        def _():
            pltpu.make_async_remote_copy(
                src_ref=s_l,
                dst_ref=r_lg.at[cc],
                send_sem=slg_sem.at[0],
                recv_sem=rlg_sem.at[cc],
                device_id=dev(me ^ 1),
                device_id_type=MESH,
            ).wait_recv()

    for t in range(R * SQ):
        here = jnp.logical_and(r_here, my_t == t)

        @pl.when(jnp.logical_not(here))
        def _():
            pltpu.make_async_remote_copy(
                src_ref=s_r,
                dst_ref=r_rg.at[t],
                send_sem=srg_sem.at[0],
                recv_sem=rrg_sem.at[t],
                device_id=dev(me ^ 1),
                device_id_type=MESH,
            ).wait_recv()

    gl = r_lg[0].astype(F32)
    for cc in range(1, C):
        gl = gl + r_lg[cc].astype(F32)
    gl = jnp.concatenate([gl[h] for h in range(GPB)], axis=1).astype(BF16)
    gr = r_rg[0].astype(F32)
    for t in range(1, R * SQ):
        gr = gr + r_rg[t].astype(F32)
    gr = gr.astype(BF16)
    repeat = zero_one(iota((M, SL), 1) == div(iota((M, SL), 0), RB))
    gr_rows = nn(repeat, gr)
    gr_rows = jnp.where(
        mod(iota((M, CP * RB), 0), RB) == mod(iota((M, CP * RB), 1), RB), gr_rows, 0.0
    ).astype(BF16)
    gr_t = nt(spread, gr_rows).astype(BF16)
    s_v[0] = nn(gl, normed_rs).astype(BF16)
    s_v[1] = nn(gr_t, normed).astype(BF16)
    send(s_v.at[1 - core], b_v, v_sem, 0, sibling)

    drain(q_w, w_sem.at[3])
    z_w[zq] = (p_w[c].astype(F32) + total(q_w, C - 1)).astype(BF16)
    send_line(z_w, w_sem, 2)

    drain(b_v, v_sem.at[1])
    p_v[c] = (s_v[core].astype(F32) + b_v[...].astype(F32)).astype(BF16)
    send_plane(p_v.at[c], p_v.at[c], v_sem, 1)

    back = zero_one(row_m == mod(col_m, SL) * RB + div(col_m, SL))
    gl_rows = nt(back, gl).astype(BF16)
    gr_cols = nt(gr_rows, spread).astype(BF16)
    ng = nn(gl_rows, lw_ref[...]) + nn(gr_cols, rw_ref[...])
    mean_grad = jnp.mean(ng, axis=1, keepdims=True)
    mean_cross = jnp.mean(ng * scaled, axis=1, keepdims=True)
    agrad_ref[...] = invstd * (ng - mean_grad - scaled * mean_cross)
    store(agrad_ref, agrad_hbm)

    drain(p_v.at[pl.ds(0, C - 1)], v_sem.at[3])
    z_v[zq] = total(p_v, C).astype(BF16)
    send_line(z_v, v_sem, 2)

    drain(z_w.at[pl.ds(0, NZ - 1)], w_sem.at[5])
    f_w[core, c] = (total(z_w, NZ) * (1.0 / residues)).astype(BF16)
    send_plane(f_w.at[core, c], f_w.at[core, c], w_sem, 3)

    pair_t = nn(w2_t, ot[...])
    pair_ref[...] = (pair_t.T + bias_ref[...]).astype(BF16)
    store(pair_ref, pair_hbm)

    drain(z_v.at[pl.ds(0, NZ - 1)], v_sem.at[5])
    f_v[core] = (total(z_v, NZ) * (1.0 / residues)).astype(BF16)
    send(f_v.at[core], f_v.at[core], v_sem, 3, sibling)

    drain(f_w.at[0, pl.ds(0, C - 1)], w_sem.at[7])
    send(f_w.at[core], f_w.at[core], w_sem, 4, sibling)

    drain(f_w.at[0], w_sem.at[9])
    store(f_w, gw_hbm)
    drain(f_v.at[0], v_sem.at[7])
    store(f_v, gv_hbm)

    drain(b_w, w_sem.at[0])
    drain(q_w, w_sem.at[2])
    drain(z_w.at[pl.ds(0, NZ - 1)], w_sem.at[4])
    drain(f_w.at[0, pl.ds(0, C - 1)], w_sem.at[6])
    drain(f_w.at[0], w_sem.at[8])
    drain(b_v, v_sem.at[0])
    drain(p_v.at[pl.ds(0, C - 1)], v_sem.at[2])
    drain(z_v.at[pl.ds(0, NZ - 1)], v_sem.at[4])
    drain(f_v.at[0], v_sem.at[6])
    for t in range(R * SQ):
        away = jnp.logical_not(jnp.logical_and(r_here, my_t == t))
        away = jnp.logical_and(away, mod(r_slot, 2) == (t // SQ) % 2)

        @pl.when(away)
        def _():
            right_copy(t).wait_send()

    for b in range(NB):
        for sq in range(SQ):
            gone = jnp.logical_and(core == b % 2, jnp.logical_not(from_sibling(b, sq)))

            @pl.when(gone)
            def _():
                hand_over(b, sq).wait_send()

    for cc in range(C):
        away = jnp.logical_not(jnp.logical_and(l_here, c == cc))

        @pl.when(away)
        def _():
            left_copy(cc).wait_send()

    for b in range(NB):
        for sq in range(SQ):
            here = jnp.logical_and(s == sq, blk == c * NB + b)

            @pl.when(jnp.logical_not(here))
            def _():
                pltpu.make_async_copy(
                    s_rg.at[b, sq], s_rg.at[b, sq], srg_sem.at[b * SQ + sq]
                ).wait()

    for k in range(NKB):
        for sq in range(SQ):
            here = jnp.logical_and(s == sq, c == s * NKB + k)

            @pl.when(jnp.logical_not(here))
            def _():
                part = s_lg.at[sq, pl.ds(k * GPB, GPB)]
                pltpu.make_async_copy(part, part, slg_sem.at[k * SQ + sq]).wait()

    for copy in stores:
        copy.wait()


def finishing(pair_in, agrad_in, gv_ref, gw_ref, pair_out, agrad_out, lwg, rwg, wog):
    pair_out[...] = pair_in[...]
    agrad_out[...] = agrad_in[...]
    CP = lwg.shape[0]
    flat = gw_ref[...].reshape(CP * CP, gw_ref.shape[-1]).astype(F32)
    for d in range(CP):
        wog[pl.ds(d, CP, stride=CP), :] = flat[d * CP : (d + 1) * CP, :]
    lwg[...] = gv_ref[0].astype(F32)
    rwg[...] = gv_ref[1].astype(F32)


def body(alignment, left_weight, right_weight, out_weight, out_bias, cotangent):
    R, C, SQ = lax.axis_size("row"), lax.axis_size("col"), lax.axis_size("seq")
    N = R * C * SQ
    SL, RB, CM = alignment.shape
    CP = left_weight.shape[1]
    CZ = out_weight.shape[1]
    rows, cols = cotangent.shape[0], cotangent.shape[1]
    dims = (R, C, SQ, SL, RB, CP, rows, cols)
    I4 = LANES // SL
    GPB, G, NKB, NB = RB // I4, rows // I4, rows // RB, cols // RB
    IJ, KS = I4 * cols, SQ * I4 * SL
    H, NZ = CP * CP // 2, R * SQ // 2
    vmem = pl.BlockSpec(memory_space=pltpu.VMEM)
    dma = pltpu.SemaphoreType.DMA
    hbm = pl.BlockSpec(memory_space=pl.ANY)
    pair, agrad, gv, gw = pl.pallas_call(
        functools.partial(kernel, dims),
        out_shape=(
            jax.ShapeDtypeStruct((rows * cols, CZ), BF16),
            jax.ShapeDtypeStruct((SL * RB, CM), F32),
            jax.ShapeDtypeStruct((2, CP, CM), BF16),
            jax.ShapeDtypeStruct((2, C, H // C, CZ), BF16),
        ),
        in_specs=[hbm] * 6,
        out_specs=(hbm,) * 4,
        scratch_shapes=[
            pltpu.VMEM((SL * RB, CM), BF16),
            pltpu.VMEM((CP, CM), BF16),
            pltpu.VMEM((CP, CM), BF16),
            pltpu.VMEM((CP * CP, CZ), BF16),
            pltpu.VMEM((1, CZ), F32),
            pltpu.VMEM((rows * cols, CZ), BF16),
            pltpu.VMEM((rows * cols, CZ), BF16),
            pltpu.VMEM((SL * RB, CM), F32),
            dma((10,)),
            pltpu.VMEM((GPB, CP, LANES), BF16),
            pltpu.VMEM((SL, CP * RB), BF16),
            pltpu.VMEM((SQ, G, CP, LANES), BF16),
            pltpu.VMEM((NB, SQ, SL, CP * RB), BF16),
            pltpu.VMEM((KS, CP * IJ), BF16),
            pltpu.VMEM((G * CP, CP * IJ), BF16),
            pltpu.VMEM((CP * CP, rows * cols), BF16),
            pltpu.VMEM((CP * CP, CZ), F32),
            pltpu.VMEM((CP * CP, CZ), BF16),
            pltpu.VMEM((SQ, G, CP, LANES), BF16),
            pltpu.VMEM((NB, SQ, SL, CP * RB), BF16),
            pltpu.VMEM((C, GPB, CP, LANES), BF16),
            pltpu.VMEM((R * SQ, SL, CP * RB), BF16),
            pltpu.VMEM((2, H, CZ), BF16),
            pltpu.VMEM((H, CZ), BF16),
            pltpu.VMEM((C, H // C, CZ), BF16),
            pltpu.VMEM((C - 1, H // C, CZ), BF16),
            pltpu.VMEM((NZ, H // C, CZ), BF16),
            pltpu.VMEM((2, C, H // C, CZ), BF16),
            pltpu.VMEM((2, CP, CM), BF16),
            pltpu.VMEM((CP, CM), BF16),
            pltpu.VMEM((C, CP, CM), BF16),
            pltpu.VMEM((NZ, CP, CM), BF16),
            pltpu.VMEM((2, CP, CM), BF16),
            dma((C,)),
            dma((NKB * SQ,)),
            dma((R * SQ,)),
            dma((NB * SQ,)),
            dma((NKB * SQ,)),
            dma((C,)),
            dma((NB * SQ,)),
            dma((R * SQ,)),
            dma((NB * SQ,)),
            dma((10,)),
            dma((8,)),
        ],
        compiler_params=pltpu.CompilerParams(
            collective_id=0, has_side_effects=True, vmem_limit_bytes=56 * 1024 * 1024
        ),
        name="outer_product_mean",
    )(
        alignment.reshape(SL * RB, CM),
        left_weight.T,
        right_weight.T,
        out_weight,
        out_bias.reshape(1, CZ),
        cotangent.reshape(rows * cols, CZ),
    )
    pair, agrad, lwg, rwg, wog = pl.pallas_call(
        finishing,
        out_shape=(
            jax.ShapeDtypeStruct(pair.shape, BF16),
            jax.ShapeDtypeStruct(agrad.shape, F32),
            jax.ShapeDtypeStruct((CP, CM), F32),
            jax.ShapeDtypeStruct((CP, CM), F32),
            jax.ShapeDtypeStruct((CP * CP, CZ), F32),
        ),
        in_specs=[vmem] * 4,
        out_specs=(vmem,) * 5,
        compiler_params=pltpu.CompilerParams(vmem_limit_bytes=56 * 1024 * 1024),
        name="finishing",
    )(pair, agrad, gv, gw)
    return (
        pair.reshape(rows, cols, CZ),
        agrad.reshape(SL, RB, CM),
        lwg.T,
        rwg.T,
        wog,
    )


def solution(mesh):
    placed = (P("seq", ("row", "col"), None), P(), P(), P(), P(), P(("row", "seq"), "col", None))
    return jax.shard_map(
        body,
        mesh=mesh,
        in_specs=placed,
        out_specs=(P(("row", "seq"), "col", None), P("seq", ("row", "col"), None), P(), P(), P()),
        check_vma=False,
    )
```

```python
import functools

import jax
import jax.numpy as jnp
from jax import lax
from jax.experimental import pallas as pl
from jax.experimental.pallas import tpu as pltpu
from jax.sharding import PartitionSpec as P

F32 = jnp.float32
BF16 = jnp.bfloat16
MESH = pl.DeviceIdType.MESH
LANES = 128
DG = 8


def nn(a, b):
    return lax.dot_general(a, b, (((1,), (0,)), ((), ())), preferred_element_type=F32)


def nt(a, b):
    return lax.dot_general(a, b, (((1,), (1,)), ((), ())), preferred_element_type=F32)


def log2(n):
    assert n & (n - 1) == 0
    return n.bit_length() - 1


def div(x, n):
    return lax.shift_right_logical(x, jnp.int32(log2(n)))


def mod(x, n):
    return x & (n - 1)


def iota(shape, dim):
    return lax.broadcasted_iota(jnp.int32, shape, dim)


def zero_one(mask):
    return jnp.where(mask, 1.0, 0.0).astype(BF16)


def kernel(
    dims,
    align_hbm,
    lw_hbm,
    rw_hbm,
    wout_hbm,
    bias_hbm,
    cot_hbm,
    pair_hbm,
    agrad_hbm,
    gv_hbm,
    gw_hbm,
    align_ref,
    lw_ref,
    rw_ref,
    wout_ref,
    bias_ref,
    cot_ref,
    pair_ref,
    agrad_ref,
    io_sem,
    s_l,
    s_r,
    l3,
    r3,
    rbd,
    og2,
    ot,
    wf,
    w2,
    s_lg,
    s_rg,
    r_lg,
    r_rg,
    s_w,
    b_w,
    p_w,
    q_w,
    z_w,
    f_w,
    s_v,
    b_v,
    p_v,
    z_v,
    f_v,
    sl_sem,
    rl_sem,
    sr_sem,
    rr_sem,
    slg_sem,
    rlg_sem,
    srg_sem,
    rrg_sem,
    w_sem,
    v_sem,
):
    R, C, SQ, SL, RB, CP, rows, cols = dims
    N = R * C * SQ
    I4 = LANES // SL
    GPB = RB // I4
    G = rows // I4
    NKB = rows // RB
    NB = cols // RB
    IJ = I4 * cols
    DH = CP // DG
    PW = DG * RB
    CH = DG * IJ
    KS = SQ * I4 * SL
    inverse = 1.0 / (SQ * SL)
    residues = RB * R * C

    r = lax.axis_index("row")
    c = lax.axis_index("col")
    s = lax.axis_index("seq")
    me = (r * C + c) * SQ + s

    def dev(lin):
        return (div(lin, C * SQ), mod(div(lin, SQ), C), mod(lin, SQ))

    loads = [
        pltpu.make_async_copy(src, dst, io_sem.at[k])
        for k, (src, dst) in enumerate(
            (
                (align_hbm, align_ref),
                (lw_hbm, lw_ref),
                (rw_hbm, rw_ref),
                (wout_hbm, wout_ref),
                (cot_hbm, cot_ref),
                (bias_hbm, bias_ref),
            )
        )
    ]
    for load in loads:
        load.start()
    stores = []

    def store(src, dst):
        stores.append(pltpu.make_async_copy(src, dst, io_sem.at[len(loads) + len(stores)]))
        stores[-1].start()

    barrier = pltpu.get_barrier_semaphore()

    def greet(k, carry):
        pl.semaphore_signal(barrier, inc=1, device_id=dev(me ^ k), device_id_type=MESH)
        return carry

    lax.fori_loop(1, N, greet, 0)

    for load in loads[:3]:
        load.wait()
    values = align_ref[...].astype(F32)
    center = values - jnp.mean(values, axis=1, keepdims=True)
    invstd = lax.rsqrt(jnp.mean(center * center, axis=1, keepdims=True) + 1e-05)
    scaled = center * invstd
    normed = scaled.astype(BF16)
    M = SL * RB
    row_m, col_m = iota((M, M), 0), iota((M, M), 1)
    perm = zero_one(col_m == mod(row_m, SL) * RB + div(row_m, SL))
    normed_rs = nn(perm, normed).astype(BF16)
    left_t = nt(lw_ref[...], normed_rs).astype(BF16)
    for h in range(GPB):
        s_l[h] = left_t[:, h * LANES : (h + 1) * LANES]
    spread = zero_one(iota((CP, CP * RB), 0) == div(iota((CP, CP * RB), 1), RB))
    CM = normed.shape[1]
    eye_m = zero_one(iota((CM, CM), 0) == iota((CM, CM), 1))
    rw_rep = nn(nt(eye_m, rw_ref[...]).astype(BF16), spread).astype(BF16)
    right_all = nn(normed_rs, rw_rep)
    lane_r = mod(iota((SL, CP * RB), 1), RB)
    right_own = jnp.zeros((SL, CP * RB), F32)
    for q in range(RB):
        right_own = jnp.where(lane_r == q, right_all[q * SL : (q + 1) * SL], right_own)
    s_r[...] = right_own.astype(BF16)

    pl.semaphore_wait(barrier, N - 1)

    l_tile, l_slot = c // NKB, c % NKB
    blk = r * C + c
    r_tile, r_slot = blk // NB, blk % NB

    def left_copy(cc):
        return pltpu.make_async_remote_copy(
            src_ref=s_l,
            dst_ref=l3.at[s, pl.ds(l_slot * GPB, GPB)],
            send_sem=sl_sem.at[0],
            recv_sem=rl_sem.at[0],
            device_id=(r, cc, l_tile),
            device_id_type=MESH,
        )

    def right_copy(t):
        return pltpu.make_async_remote_copy(
            src_ref=s_r,
            dst_ref=r3.at[r_slot, s],
            send_sem=sr_sem.at[0],
            recv_sem=rr_sem.at[0],
            device_id=(t // SQ, r_tile, t % SQ),
            device_id_type=MESH,
        )

    l_here = l_tile == s
    r_here = r_tile == c

    def drain(ref, sem):
        pltpu.make_async_copy(ref, ref, sem).wait()

    def drain_blocks(count, sem, here):
        @pl.when(here)
        def _():
            drain(r_rg.at[pl.ds(0, count - 1)], sem.at[0])

        @pl.when(jnp.logical_not(here))
        def _():
            drain(r_rg.at[pl.ds(0, count)], sem.at[0])

    my_t = r * SQ + s
    for t in range(R * SQ):
        away = jnp.logical_not(jnp.logical_and(r_here, my_t == t))

        @pl.when(away)
        def _():
            right_copy(t).start()

    for cc in range(C):
        away = jnp.logical_not(jnp.logical_and(l_here, c == cc))

        @pl.when(away)
        def _():
            left_copy(cc).start()

    @pl.when(r_here)
    def _():
        r3[r_slot, s] = s_r[...]

    @pl.when(l_here)
    def _():
        l3[s, pl.ds(l_slot * GPB, GPB)] = s_l[...]

    for load in loads[3:]:
        load.wait()
    wf[...] = wout_ref[...].astype(F32)
    for d in range(CP):
        w2[d * CP : (d + 1) * CP, :] = wf[pl.ds(d, CP, stride=CP), :].astype(BF16)
    cot = cot_ref[...]
    eye_z = zero_one(iota((LANES, LANES), 0) == iota((LANES, LANES), 1))
    w2_t = nt(eye_z, w2[...]).astype(BF16)
    for dh in range(DH):
        part = nt(w2[dh * DG * CP : (dh + 1) * DG * CP, :], cot) * inverse
        part = part.astype(BF16)
        for d in range(DG):
            for g in range(G):
                og2[g * CP : (g + 1) * CP, dh * CH + d * IJ : dh * CH + (d + 1) * IJ] = part[
                    d * CP : (d + 1) * CP, g * IJ : (g + 1) * IJ
                ]
    fr, fc = iota((NB * PW, CH), 0), iota((NB * PW, CH), 1)
    fold = zero_one(
        fr == mod(div(fc, RB), NB) * PW + div(fc, IJ) * RB + mod(fc, RB)
    )
    i_lane = mod(div(iota((SL, CH), 1), cols), I4)

    drain_blocks(NKB * SQ, rl_sem, l_here)

    left = jnp.concatenate([l3[sq].reshape(G * CP, LANES) for sq in range(SQ)], axis=1)
    eye_k = zero_one(iota((KS, KS), 0) == iota((KS, KS), 1))
    left_turned = nt(eye_k, left).astype(BF16)
    folded = []
    for dh in range(DH):
        z = nn(left_turned, og2[:, dh * CH : (dh + 1) * CH])
        picked = []
        for sq in range(SQ):
            y = z[sq * I4 * SL : (sq * I4 + 1) * SL]
            for i in range(1, I4):
                start = (sq * I4 + i) * SL
                y = jnp.where(i_lane == i, z[start : start + SL], y)
            picked.append(y)
        folded.append(nt(jnp.concatenate(picked, axis=0).astype(BF16), fold))
    for b in range(NB):
        for sq in range(SQ):
            s_rg[b, sq] = jnp.concatenate(
                [f[sq * SL : (sq + 1) * SL, b * PW : (b + 1) * PW] for f in folded], axis=1
            ).astype(BF16)
    for b in range(NB):
        for sq in range(SQ):
            owner = c * NB + b
            here = jnp.logical_and(s == sq, blk == owner)

            @pl.when(jnp.logical_not(here))
            def _():
                pltpu.make_async_remote_copy(
                    src_ref=s_rg.at[b, sq],
                    dst_ref=r_rg.at[my_t],
                    send_sem=srg_sem.at[0],
                    recv_sem=rrg_sem.at[0],
                    device_id=(owner // C, owner % C, sq),
                    device_id_type=MESH,
                ).start()

            @pl.when(here)
            def _():
                r_rg[my_t] = s_rg[b, sq]

    drain_blocks(NB * SQ, rr_sem, r_here)

    for dh in range(DH):
        gathered = jnp.concatenate(
            [
                jnp.concatenate(
                    [r3[b, sq][:, dh * PW : (dh + 1) * PW] for b in range(NB)], axis=1
                )
                for sq in range(SQ)
            ],
            axis=0,
        )
        wide = nn(gathered, fold)
        for sq in range(SQ):
            for i in range(I4):
                start = (sq * I4 + i) * SL
                rbd[start : start + SL, dh * CH : (dh + 1) * CH] = jnp.where(
                    i_lane == i, wide[sq * SL : (sq + 1) * SL], 0.0
                ).astype(BF16)

    lg = nt(og2[...], rbd[...]).astype(BF16)
    for sq in range(SQ):
        for g in range(G):
            s_lg[sq, g] = lg[g * CP : (g + 1) * CP, sq * LANES : (sq + 1) * LANES]
    for k in range(NKB):
        for sq in range(SQ):
            here = jnp.logical_and(s == sq, c == s * NKB + k)

            @pl.when(jnp.logical_not(here))
            def _():
                pltpu.make_async_remote_copy(
                    src_ref=s_lg.at[sq, pl.ds(k * GPB, GPB)],
                    dst_ref=r_lg.at[c],
                    send_sem=slg_sem.at[0],
                    recv_sem=rlg_sem.at[0],
                    device_id=(r, s * NKB + k, sq),
                    device_id_type=MESH,
                ).start()

            @pl.when(here)
            def _():
                r_lg[c] = s_lg[sq, pl.ds(k * GPB, GPB)]

    for dh in range(DH):
        part = nn(left, rbd[:, dh * CH : (dh + 1) * CH]) * inverse
        part = part.astype(BF16)
        for d in range(DG):
            for g in range(G):
                start = (dh * DG + d) * CP
                ot[start : start + CP, g * IJ : (g + 1) * IJ] = part[
                    g * CP : (g + 1) * CP, d * IJ : (d + 1) * IJ
                ]

    core = mod(r, 2)
    sibling = (r ^ 1, c, s)
    NZ = R * SQ // 2
    zq = div(r, 2) * SQ + s

    def send(src, dst, sems, phase, target):
        pltpu.make_async_remote_copy(
            src_ref=src,
            dst_ref=dst,
            send_sem=sems.at[2 * phase],
            recv_sem=sems.at[2 * phase + 1],
            device_id=target,
            device_id_type=MESH,
        ).start()

    def send_plane(src, dst, sems, phase):
        for k in range(1, C):
            send(src, dst, sems, phase, (r, c ^ k, s))

    def send_line(ref, sems, phase):
        for k in range(1, NZ):
            other = zq ^ k
            send(
                ref.at[zq],
                ref.at[zq],
                sems,
                phase,
                (div(other, SQ) * 2 + core, c, mod(other, SQ)),
            )

    def total(ref, count):
        out = ref[0].astype(F32)
        for k in range(1, count):
            out = out + ref[k].astype(F32)
        return out

    wo = nn(ot[...], cot)
    s_w[...] = wo.astype(BF16).reshape(s_w.shape)
    send(s_w.at[1 - core], b_w, w_sem, 0, sibling)

    drain(b_w, w_sem.at[1])
    p_w[...] = (s_w[core].astype(F32) + b_w[...].astype(F32)).astype(BF16).reshape(p_w.shape)
    for k in range(1, C):
        send(p_w.at[c ^ k], q_w.at[k - 1], w_sem, 1, (r, c ^ k, s))

    drain_blocks(C, rlg_sem, l_here)
    drain_blocks(R * SQ, rrg_sem, r_here)

    gl = r_lg[0].astype(F32)
    for cc in range(1, C):
        gl = gl + r_lg[cc].astype(F32)
    gl = jnp.concatenate([gl[h] for h in range(GPB)], axis=1).astype(BF16)
    gr = r_rg[0].astype(F32)
    for t in range(1, R * SQ):
        gr = gr + r_rg[t].astype(F32)
    gr = gr.astype(BF16)
    repeat = zero_one(iota((M, SL), 1) == div(iota((M, SL), 0), RB))
    gr_rows = nn(repeat, gr)
    gr_rows = jnp.where(
        mod(iota((M, CP * RB), 0), RB) == mod(iota((M, CP * RB), 1), RB), gr_rows, 0.0
    ).astype(BF16)
    gr_t = nt(spread, gr_rows).astype(BF16)
    s_v[0] = nn(gl, normed_rs).astype(BF16)
    s_v[1] = nn(gr_t, normed).astype(BF16)
    send(s_v.at[1 - core], b_v, v_sem, 0, sibling)

    drain(q_w, w_sem.at[3])
    z_w[zq] = (p_w[c].astype(F32) + total(q_w, C - 1)).astype(BF16)
    send_line(z_w, w_sem, 2)

    drain(b_v, v_sem.at[1])
    p_v[c] = (s_v[core].astype(F32) + b_v[...].astype(F32)).astype(BF16)
    send_plane(p_v.at[c], p_v.at[c], v_sem, 1)

    back = zero_one(row_m == mod(col_m, SL) * RB + div(col_m, SL))
    gl_rows = nt(back, gl).astype(BF16)
    gr_cols = nt(gr_rows, spread).astype(BF16)
    ng = nn(gl_rows, lw_ref[...]) + nn(gr_cols, rw_ref[...])
    mean_grad = jnp.mean(ng, axis=1, keepdims=True)
    mean_cross = jnp.mean(ng * scaled, axis=1, keepdims=True)
    agrad_ref[...] = invstd * (ng - mean_grad - scaled * mean_cross)
    store(agrad_ref, agrad_hbm)

    drain(p_v.at[pl.ds(0, C - 1)], v_sem.at[3])
    z_v[zq] = total(p_v, C).astype(BF16)
    send_line(z_v, v_sem, 2)

    drain(z_w.at[pl.ds(0, NZ - 1)], w_sem.at[5])
    f_w[core, c] = (total(z_w, NZ) * (1.0 / residues)).astype(BF16)
    send_plane(f_w.at[core, c], f_w.at[core, c], w_sem, 3)

    pair_t = nn(w2_t, ot[...])
    pair_ref[...] = (pair_t.T + bias_ref[...]).astype(BF16)
    store(pair_ref, pair_hbm)

    drain(z_v.at[pl.ds(0, NZ - 1)], v_sem.at[5])
    f_v[core] = (total(z_v, NZ) * (1.0 / residues)).astype(BF16)
    send(f_v.at[core], f_v.at[core], v_sem, 3, sibling)

    drain(f_w.at[0, pl.ds(0, C - 1)], w_sem.at[7])
    send(f_w.at[core], f_w.at[core], w_sem, 4, sibling)

    drain_blocks(C, sl_sem, l_here)
    drain_blocks(R * SQ, sr_sem, r_here)
    drain_blocks(NKB * SQ, slg_sem, l_here)
    drain_blocks(NB * SQ, srg_sem, r_here)
    drain(b_w, w_sem.at[0])
    drain(q_w, w_sem.at[2])
    drain(z_w.at[pl.ds(0, NZ - 1)], w_sem.at[4])
    drain(f_w.at[0, pl.ds(0, C - 1)], w_sem.at[6])
    drain(b_v, v_sem.at[0])
    drain(p_v.at[pl.ds(0, C - 1)], v_sem.at[2])
    drain(z_v.at[pl.ds(0, NZ - 1)], v_sem.at[4])

    drain(f_w.at[0], w_sem.at[9])
    store(f_w, gw_hbm)
    drain(f_v.at[0], v_sem.at[7])
    store(f_v, gv_hbm)

    drain(f_w.at[0], w_sem.at[8])
    drain(f_v.at[0], v_sem.at[6])
    for copy in stores:
        copy.wait()


def finishing(pair_in, agrad_in, gv_ref, gw_ref, pair_out, agrad_out, lwg, rwg, wog):
    pair_out[...] = pair_in[...]
    agrad_out[...] = agrad_in[...]
    CP = lwg.shape[0]
    flat = gw_ref[...].reshape(CP * CP, gw_ref.shape[-1]).astype(F32)
    for d in range(CP):
        wog[pl.ds(d, CP, stride=CP), :] = flat[d * CP : (d + 1) * CP, :]
    lwg[...] = gv_ref[0].astype(F32)
    rwg[...] = gv_ref[1].astype(F32)


def body(alignment, left_weight, right_weight, out_weight, out_bias, cotangent):
    R, C, SQ = lax.axis_size("row"), lax.axis_size("col"), lax.axis_size("seq")
    N = R * C * SQ
    SL, RB, CM = alignment.shape
    CP = left_weight.shape[1]
    CZ = out_weight.shape[1]
    rows, cols = cotangent.shape[0], cotangent.shape[1]
    dims = (R, C, SQ, SL, RB, CP, rows, cols)
    I4 = LANES // SL
    GPB, G, NKB, NB = RB // I4, rows // I4, rows // RB, cols // RB
    IJ, KS = I4 * cols, SQ * I4 * SL
    H, NZ = CP * CP // 2, R * SQ // 2
    vmem = pl.BlockSpec(memory_space=pltpu.VMEM)
    dma = pltpu.SemaphoreType.DMA
    hbm = pl.BlockSpec(memory_space=pl.ANY)
    pair, agrad, gv, gw = pl.pallas_call(
        functools.partial(kernel, dims),
        out_shape=(
            jax.ShapeDtypeStruct((rows * cols, CZ), BF16),
            jax.ShapeDtypeStruct((SL * RB, CM), F32),
            jax.ShapeDtypeStruct((2, CP, CM), BF16),
            jax.ShapeDtypeStruct((2, C, H // C, CZ), BF16),
        ),
        in_specs=[hbm] * 6,
        out_specs=(hbm,) * 4,
        scratch_shapes=[
            pltpu.VMEM((SL * RB, CM), BF16),
            pltpu.VMEM((CP, CM), BF16),
            pltpu.VMEM((CP, CM), BF16),
            pltpu.VMEM((CP * CP, CZ), BF16),
            pltpu.VMEM((1, CZ), F32),
            pltpu.VMEM((rows * cols, CZ), BF16),
            pltpu.VMEM((rows * cols, CZ), BF16),
            pltpu.VMEM((SL * RB, CM), F32),
            dma((10,)),
            pltpu.VMEM((GPB, CP, LANES), BF16),
            pltpu.VMEM((SL, CP * RB), BF16),
            pltpu.VMEM((SQ, G, CP, LANES), BF16),
            pltpu.VMEM((NB, SQ, SL, CP * RB), BF16),
            pltpu.VMEM((KS, CP * IJ), BF16),
            pltpu.VMEM((G * CP, CP * IJ), BF16),
            pltpu.VMEM((CP * CP, rows * cols), BF16),
            pltpu.VMEM((CP * CP, CZ), F32),
            pltpu.VMEM((CP * CP, CZ), BF16),
            pltpu.VMEM((SQ, G, CP, LANES), BF16),
            pltpu.VMEM((NB, SQ, SL, CP * RB), BF16),
            pltpu.VMEM((C, GPB, CP, LANES), BF16),
            pltpu.VMEM((R * SQ, SL, CP * RB), BF16),
            pltpu.VMEM((2, H, CZ), BF16),
            pltpu.VMEM((H, CZ), BF16),
            pltpu.VMEM((C, H // C, CZ), BF16),
            pltpu.VMEM((C - 1, H // C, CZ), BF16),
            pltpu.VMEM((NZ, H // C, CZ), BF16),
            pltpu.VMEM((2, C, H // C, CZ), BF16),
            pltpu.VMEM((2, CP, CM), BF16),
            pltpu.VMEM((CP, CM), BF16),
            pltpu.VMEM((C, CP, CM), BF16),
            pltpu.VMEM((NZ, CP, CM), BF16),
            pltpu.VMEM((2, CP, CM), BF16),
            dma((1,)),
            dma((1,)),
            dma((1,)),
            dma((1,)),
            dma((1,)),
            dma((1,)),
            dma((1,)),
            dma((1,)),
            dma((10,)),
            dma((8,)),
        ],
        compiler_params=pltpu.CompilerParams(
            collective_id=0, has_side_effects=True, vmem_limit_bytes=56 * 1024 * 1024
        ),
        name="outer_product_mean",
    )(
        alignment.reshape(SL * RB, CM),
        left_weight.T,
        right_weight.T,
        out_weight,
        out_bias.reshape(1, CZ),
        cotangent.reshape(rows * cols, CZ),
    )
    pair, agrad, lwg, rwg, wog = pl.pallas_call(
        finishing,
        out_shape=(
            jax.ShapeDtypeStruct(pair.shape, BF16),
            jax.ShapeDtypeStruct(agrad.shape, F32),
            jax.ShapeDtypeStruct((CP, CM), F32),
            jax.ShapeDtypeStruct((CP, CM), F32),
            jax.ShapeDtypeStruct((CP * CP, CZ), F32),
        ),
        in_specs=[vmem] * 4,
        out_specs=(vmem,) * 5,
        compiler_params=pltpu.CompilerParams(vmem_limit_bytes=56 * 1024 * 1024),
        name="finishing",
    )(pair, agrad, gv, gw)
    return (
        pair.reshape(rows, cols, CZ),
        agrad.reshape(SL, RB, CM),
        lwg.T,
        rwg.T,
        wog,
    )


def solution(mesh):
    placed = (P("seq", ("row", "col"), None), P(), P(), P(), P(), P(("row", "seq"), "col", None))
    return jax.shard_map(
        body,
        mesh=mesh,
        in_specs=placed,
        out_specs=(P(("row", "seq"), "col", None), P("seq", ("row", "col"), None), P(), P(), P()),
        check_vma=False,
    )
```

```python
import functools

import jax
import jax.numpy as jnp
from jax import lax
from jax.experimental import pallas as pl
from jax.experimental.pallas import tpu as pltpu
from jax.sharding import PartitionSpec as P

F32 = jnp.float32
BF16 = jnp.bfloat16
MESH = pl.DeviceIdType.MESH
LANES = 128
DG = 8


def nn(a, b):
    return lax.dot_general(a, b, (((1,), (0,)), ((), ())), preferred_element_type=F32)


def nt(a, b):
    return lax.dot_general(a, b, (((1,), (1,)), ((), ())), preferred_element_type=F32)


def log2(n):
    assert n & (n - 1) == 0
    return n.bit_length() - 1


def div(x, n):
    return lax.shift_right_logical(x, jnp.int32(log2(n)))


def mod(x, n):
    return x & (n - 1)


def iota(shape, dim):
    return lax.broadcasted_iota(jnp.int32, shape, dim)


def zero_one(mask):
    return jnp.where(mask, 1.0, 0.0).astype(BF16)


def kernel(
    dims,
    align_hbm,
    lw_hbm,
    rw_hbm,
    wout_hbm,
    bias_hbm,
    cot_hbm,
    pair_hbm,
    agrad_hbm,
    gv_hbm,
    gw_hbm,
    align_ref,
    lw_ref,
    rw_ref,
    wout_ref,
    bias_ref,
    cot_ref,
    pair_ref,
    agrad_ref,
    io_sem,
    s_l,
    s_r,
    l3,
    r3,
    rbd,
    og2,
    ot,
    wf,
    w2,
    s_lg,
    s_rg,
    r_lg,
    r_rg,
    s_w,
    b_w,
    p_w,
    q_w,
    z_w,
    f_w,
    s_v,
    b_v,
    p_v,
    z_v,
    f_v,
    sl_sem,
    rl_sem,
    sr_sem,
    rr_sem,
    slg_sem,
    rlg_sem,
    srg_sem,
    rrg_sem,
    w_sem,
    v_sem,
):
    R, C, SQ, SL, RB, CP, rows, cols = dims
    N = R * C * SQ
    I4 = LANES // SL
    GPB = RB // I4
    G = rows // I4
    NKB = rows // RB
    NB = cols // RB
    IJ = I4 * cols
    DH = CP // DG
    PW = DG * RB
    CH = DG * IJ
    KS = SQ * I4 * SL
    inverse = 1.0 / (SQ * SL)
    residues = RB * R * C

    r = lax.axis_index("row")
    c = lax.axis_index("col")
    s = lax.axis_index("seq")
    me = (r * C + c) * SQ + s

    def dev(lin):
        return (div(lin, C * SQ), mod(div(lin, SQ), C), mod(lin, SQ))

    loads = [
        pltpu.make_async_copy(src, dst, io_sem.at[k])
        for k, (src, dst) in enumerate(
            (
                (align_hbm, align_ref),
                (lw_hbm, lw_ref),
                (rw_hbm, rw_ref),
                (wout_hbm, wout_ref),
                (cot_hbm, cot_ref),
                (bias_hbm, bias_ref),
            )
        )
    ]
    for load in loads:
        load.start()
    stores = []

    def store(src, dst):
        stores.append(pltpu.make_async_copy(src, dst, io_sem.at[len(loads) + len(stores)]))
        stores[-1].start()

    barrier = pltpu.get_barrier_semaphore()

    def greet(k, carry):
        pl.semaphore_signal(barrier, inc=1, device_id=dev(me ^ k), device_id_type=MESH)
        return carry

    lax.fori_loop(1, N, greet, 0)

    for load in loads[:3]:
        load.wait()
    values = align_ref[...].astype(F32)
    center = values - jnp.mean(values, axis=1, keepdims=True)
    invstd = lax.rsqrt(jnp.mean(center * center, axis=1, keepdims=True) + 1e-05)
    scaled = center * invstd
    normed = scaled.astype(BF16)
    M = SL * RB
    row_m, col_m = iota((M, M), 0), iota((M, M), 1)
    perm = zero_one(col_m == mod(row_m, SL) * RB + div(row_m, SL))
    normed_rs = nn(perm, normed).astype(BF16)
    left_t = nt(lw_ref[...], normed_rs).astype(BF16)
    for h in range(GPB):
        s_l[h] = left_t[:, h * LANES : (h + 1) * LANES]
    spread = zero_one(iota((CP, CP * RB), 0) == div(iota((CP, CP * RB), 1), RB))
    CM = normed.shape[1]
    eye_m = zero_one(iota((CM, CM), 0) == iota((CM, CM), 1))
    rw_rep = nn(nt(eye_m, rw_ref[...]).astype(BF16), spread).astype(BF16)
    right_all = nn(normed_rs, rw_rep)
    lane_r = mod(iota((SL, CP * RB), 1), RB)
    right_own = jnp.zeros((SL, CP * RB), F32)
    for q in range(RB):
        right_own = jnp.where(lane_r == q, right_all[q * SL : (q + 1) * SL], right_own)
    s_r[...] = right_own.astype(BF16)

    pl.semaphore_wait(barrier, N - 1)

    l_tile, l_slot = c // NKB, c % NKB
    blk = r * C + c
    r_tile, r_slot = blk // NB, blk % NB

    def left_copy(cc):
        return pltpu.make_async_remote_copy(
            src_ref=s_l,
            dst_ref=l3.at[s, pl.ds(l_slot * GPB, GPB)],
            send_sem=sl_sem.at[0],
            recv_sem=rl_sem.at[0],
            device_id=(r, cc, l_tile),
            device_id_type=MESH,
        )

    def right_copy(t):
        return pltpu.make_async_remote_copy(
            src_ref=s_r,
            dst_ref=r3.at[r_slot, s],
            send_sem=sr_sem.at[0],
            recv_sem=rr_sem.at[0],
            device_id=(t // SQ, r_tile, t % SQ),
            device_id_type=MESH,
        )

    l_here = l_tile == s
    r_here = r_tile == c

    def drain(ref, sem):
        pltpu.make_async_copy(ref, ref, sem).wait()

    def drain_blocks(count, sem, here):
        @pl.when(here)
        def _():
            drain(r_rg.at[pl.ds(0, count - 1)], sem.at[0])

        @pl.when(jnp.logical_not(here))
        def _():
            drain(r_rg.at[pl.ds(0, count)], sem.at[0])

    my_t = r * SQ + s
    for t in range(R * SQ):
        away = jnp.logical_not(jnp.logical_and(r_here, my_t == t))

        @pl.when(away)
        def _():
            right_copy(t).start()

    for cc in range(C):
        away = jnp.logical_not(jnp.logical_and(l_here, c == cc))

        @pl.when(away)
        def _():
            left_copy(cc).start()

    @pl.when(r_here)
    def _():
        r3[r_slot, s] = s_r[...]

    @pl.when(l_here)
    def _():
        l3[s, pl.ds(l_slot * GPB, GPB)] = s_l[...]

    for load in loads[3:]:
        load.wait()
    wf[...] = wout_ref[...].astype(F32)
    for d in range(CP):
        w2[d * CP : (d + 1) * CP, :] = wf[pl.ds(d, CP, stride=CP), :].astype(BF16)
    cot = cot_ref[...]
    eye_z = zero_one(iota((LANES, LANES), 0) == iota((LANES, LANES), 1))
    w2_t = nt(eye_z, w2[...]).astype(BF16)
    for dh in range(DH):
        part = nt(w2[dh * DG * CP : (dh + 1) * DG * CP, :], cot) * inverse
        part = part.astype(BF16)
        for d in range(DG):
            for g in range(G):
                og2[g * CP : (g + 1) * CP, dh * CH + d * IJ : dh * CH + (d + 1) * IJ] = part[
                    d * CP : (d + 1) * CP, g * IJ : (g + 1) * IJ
                ]
    fr, fc = iota((NB * PW, CH), 0), iota((NB * PW, CH), 1)
    fold = zero_one(
        fr == mod(div(fc, RB), NB) * PW + div(fc, IJ) * RB + mod(fc, RB)
    )
    i_lane = mod(div(iota((SL, CH), 1), cols), I4)

    drain_blocks(NKB * SQ, rl_sem, l_here)

    left = jnp.concatenate([l3[sq].reshape(G * CP, LANES) for sq in range(SQ)], axis=1)
    eye_k = zero_one(iota((KS, KS), 0) == iota((KS, KS), 1))
    left_turned = nt(eye_k, left).astype(BF16)
    folded = []
    for dh in range(DH):
        z = nn(left_turned, og2[:, dh * CH : (dh + 1) * CH])
        picked = []
        for sq in range(SQ):
            y = z[sq * I4 * SL : (sq * I4 + 1) * SL]
            for i in range(1, I4):
                start = (sq * I4 + i) * SL
                y = jnp.where(i_lane == i, z[start : start + SL], y)
            picked.append(y)
        folded.append(nt(jnp.concatenate(picked, axis=0).astype(BF16), fold))
    for b in range(NB):
        for sq in range(SQ):
            s_rg[b, sq] = jnp.concatenate(
                [f[sq * SL : (sq + 1) * SL, b * PW : (b + 1) * PW] for f in folded], axis=1
            ).astype(BF16)
    for b in range(NB):
        for sq in range(SQ):
            owner = c * NB + b
            here = jnp.logical_and(s == sq, blk == owner)

            @pl.when(jnp.logical_not(here))
            def _():
                pltpu.make_async_remote_copy(
                    src_ref=s_rg.at[b, sq],
                    dst_ref=r_rg.at[my_t],
                    send_sem=srg_sem.at[0],
                    recv_sem=rrg_sem.at[0],
                    device_id=(owner // C, owner % C, sq),
                    device_id_type=MESH,
                ).start()

            @pl.when(here)
            def _():
                r_rg[my_t] = s_rg[b, sq]

    drain_blocks(NB * SQ, rr_sem, r_here)

    for dh in range(DH):
        gathered = jnp.concatenate(
            [
                jnp.concatenate(
                    [r3[b, sq][:, dh * PW : (dh + 1) * PW] for b in range(NB)], axis=1
                )
                for sq in range(SQ)
            ],
            axis=0,
        )
        wide = nn(gathered, fold)
        for sq in range(SQ):
            for i in range(I4):
                start = (sq * I4 + i) * SL
                rbd[start : start + SL, dh * CH : (dh + 1) * CH] = jnp.where(
                    i_lane == i, wide[sq * SL : (sq + 1) * SL], 0.0
                ).astype(BF16)

    lg = nt(og2[...], rbd[...]).astype(BF16)
    for sq in range(SQ):
        for g in range(G):
            s_lg[sq, g] = lg[g * CP : (g + 1) * CP, sq * LANES : (sq + 1) * LANES]
    for k in range(NKB):
        for sq in range(SQ):
            here = jnp.logical_and(s == sq, c == s * NKB + k)

            @pl.when(jnp.logical_not(here))
            def _():
                pltpu.make_async_remote_copy(
                    src_ref=s_lg.at[sq, pl.ds(k * GPB, GPB)],
                    dst_ref=r_lg.at[c],
                    send_sem=slg_sem.at[0],
                    recv_sem=rlg_sem.at[0],
                    device_id=(r, s * NKB + k, sq),
                    device_id_type=MESH,
                ).start()

            @pl.when(here)
            def _():
                r_lg[c] = s_lg[sq, pl.ds(k * GPB, GPB)]

    for dh in range(DH):
        part = nn(left, rbd[:, dh * CH : (dh + 1) * CH]) * inverse
        part = part.astype(BF16)
        for d in range(DG):
            for g in range(G):
                start = (dh * DG + d) * CP
                ot[start : start + CP, g * IJ : (g + 1) * IJ] = part[
                    g * CP : (g + 1) * CP, d * IJ : (d + 1) * IJ
                ]

    core = mod(r, 2)
    sibling = (r ^ 1, c, s)
    NZ = R * SQ // 2
    zq = div(r, 2) * SQ + s

    def send(src, dst, sems, phase, target):
        pltpu.make_async_remote_copy(
            src_ref=src,
            dst_ref=dst,
            send_sem=sems.at[2 * phase],
            recv_sem=sems.at[2 * phase + 1],
            device_id=target,
            device_id_type=MESH,
        ).start()

    def send_plane(src, dst, sems, phase):
        for k in range(1, C):
            send(src, dst, sems, phase, (r, c ^ k, s))

    def send_line(ref, sems, phase):
        for k in range(1, NZ):
            other = zq ^ k
            send(
                ref.at[zq],
                ref.at[zq],
                sems,
                phase,
                (div(other, SQ) * 2 + core, c, mod(other, SQ)),
            )

    def total(ref, count):
        out = ref[0].astype(F32)
        for k in range(1, count):
            out = out + ref[k].astype(F32)
        return out

    H = s_w.shape[1]

    def half(which):
        start = pl.multiple_of(which * H, H)
        s_w[which] = nn(ot[pl.ds(start, H), :], cot).astype(BF16)

    half(1 - core)
    send(s_w.at[1 - core], b_w, w_sem, 0, sibling)
    half(core)

    pair_t = nn(w2_t, ot[...])
    pair_ref[...] = (pair_t.T + bias_ref[...]).astype(BF16)
    store(pair_ref, pair_hbm)

    drain(b_w, w_sem.at[1])
    p_w[...] = (s_w[core].astype(F32) + b_w[...].astype(F32)).astype(BF16).reshape(p_w.shape)
    for k in range(1, C):
        send(p_w.at[c ^ k], q_w.at[k - 1], w_sem, 1, (r, c ^ k, s))

    drain_blocks(R * SQ, rrg_sem, r_here)

    gr = r_rg[0].astype(F32)
    for t in range(1, R * SQ):
        gr = gr + r_rg[t].astype(F32)
    gr = gr.astype(BF16)
    repeat = zero_one(iota((M, SL), 1) == div(iota((M, SL), 0), RB))
    gr_rows = nn(repeat, gr)
    gr_rows = jnp.where(
        mod(iota((M, CP * RB), 0), RB) == mod(iota((M, CP * RB), 1), RB), gr_rows, 0.0
    ).astype(BF16)
    gr_t = nt(spread, gr_rows).astype(BF16)
    s_v[1] = nn(gr_t, normed).astype(BF16)
    drain_blocks(C, rlg_sem, l_here)
    gl = r_lg[0].astype(F32)
    for cc in range(1, C):
        gl = gl + r_lg[cc].astype(F32)
    gl = jnp.concatenate([gl[h] for h in range(GPB)], axis=1).astype(BF16)
    s_v[0] = nn(gl, normed_rs).astype(BF16)
    send(s_v.at[1 - core], b_v, v_sem, 0, sibling)

    drain(q_w, w_sem.at[3])
    z_w[zq] = (p_w[c].astype(F32) + total(q_w, C - 1)).astype(BF16)
    send_line(z_w, w_sem, 2)

    drain(b_v, v_sem.at[1])
    p_v[c] = (s_v[core].astype(F32) + b_v[...].astype(F32)).astype(BF16)
    send_plane(p_v.at[c], p_v.at[c], v_sem, 1)

    back = zero_one(row_m == mod(col_m, SL) * RB + div(col_m, SL))
    gl_rows = nt(back, gl).astype(BF16)
    gr_cols = nt(gr_rows, spread).astype(BF16)
    ng = nn(gl_rows, lw_ref[...]) + nn(gr_cols, rw_ref[...])
    mean_grad = jnp.mean(ng, axis=1, keepdims=True)
    mean_cross = jnp.mean(ng * scaled, axis=1, keepdims=True)
    agrad_ref[...] = invstd * (ng - mean_grad - scaled * mean_cross)
    store(agrad_ref, agrad_hbm)

    drain(p_v.at[pl.ds(0, C - 1)], v_sem.at[3])
    z_v[zq] = total(p_v, C).astype(BF16)
    send_line(z_v, v_sem, 2)

    drain(z_w.at[pl.ds(0, NZ - 1)], w_sem.at[5])
    f_w[core, c] = (total(z_w, NZ) * (1.0 / residues)).astype(BF16)
    send_plane(f_w.at[core, c], f_w.at[core, c], w_sem, 3)

    drain(z_v.at[pl.ds(0, NZ - 1)], v_sem.at[5])
    f_v[core] = (total(z_v, NZ) * (1.0 / residues)).astype(BF16)
    send(f_v.at[core], f_v.at[core], v_sem, 3, sibling)

    drain(f_w.at[0, pl.ds(0, C - 1)], w_sem.at[7])
    send(f_w.at[core], f_w.at[core], w_sem, 4, sibling)

    drain_blocks(C, sl_sem, l_here)
    drain_blocks(R * SQ, sr_sem, r_here)
    drain_blocks(NKB * SQ, slg_sem, l_here)
    drain_blocks(NB * SQ, srg_sem, r_here)
    drain(b_w, w_sem.at[0])
    drain(q_w, w_sem.at[2])
    drain(z_w.at[pl.ds(0, NZ - 1)], w_sem.at[4])
    drain(f_w.at[0, pl.ds(0, C - 1)], w_sem.at[6])
    drain(b_v, v_sem.at[0])
    drain(p_v.at[pl.ds(0, C - 1)], v_sem.at[2])
    drain(z_v.at[pl.ds(0, NZ - 1)], v_sem.at[4])

    drain(f_w.at[0], w_sem.at[9])
    store(f_w, gw_hbm)
    drain(f_v.at[0], v_sem.at[7])
    store(f_v, gv_hbm)

    drain(f_w.at[0], w_sem.at[8])
    drain(f_v.at[0], v_sem.at[6])
    for copy in stores:
        copy.wait()


def finishing(pair_in, agrad_in, gv_ref, gw_ref, pair_out, agrad_out, lwg, rwg, wog):
    pair_out[...] = pair_in[...]
    agrad_out[...] = agrad_in[...]
    CP = lwg.shape[0]
    flat = gw_ref[...].reshape(CP * CP, gw_ref.shape[-1]).astype(F32)
    for d in range(CP):
        wog[pl.ds(d, CP, stride=CP), :] = flat[d * CP : (d + 1) * CP, :]
    lwg[...] = gv_ref[0].astype(F32)
    rwg[...] = gv_ref[1].astype(F32)


def body(alignment, left_weight, right_weight, out_weight, out_bias, cotangent):
    R, C, SQ = lax.axis_size("row"), lax.axis_size("col"), lax.axis_size("seq")
    N = R * C * SQ
    SL, RB, CM = alignment.shape
    CP = left_weight.shape[1]
    CZ = out_weight.shape[1]
    rows, cols = cotangent.shape[0], cotangent.shape[1]
    dims = (R, C, SQ, SL, RB, CP, rows, cols)
    I4 = LANES // SL
    GPB, G, NKB, NB = RB // I4, rows // I4, rows // RB, cols // RB
    IJ, KS = I4 * cols, SQ * I4 * SL
    H, NZ = CP * CP // 2, R * SQ // 2
    vmem = pl.BlockSpec(memory_space=pltpu.VMEM)
    dma = pltpu.SemaphoreType.DMA
    hbm = pl.BlockSpec(memory_space=pl.ANY)
    pair, agrad, gv, gw = pl.pallas_call(
        functools.partial(kernel, dims),
        out_shape=(
            jax.ShapeDtypeStruct((rows * cols, CZ), BF16),
            jax.ShapeDtypeStruct((SL * RB, CM), F32),
            jax.ShapeDtypeStruct((2, CP, CM), BF16),
            jax.ShapeDtypeStruct((2, C, H // C, CZ), BF16),
        ),
        in_specs=[hbm] * 6,
        out_specs=(hbm,) * 4,
        scratch_shapes=[
            pltpu.VMEM((SL * RB, CM), BF16),
            pltpu.VMEM((CP, CM), BF16),
            pltpu.VMEM((CP, CM), BF16),
            pltpu.VMEM((CP * CP, CZ), BF16),
            pltpu.VMEM((1, CZ), F32),
            pltpu.VMEM((rows * cols, CZ), BF16),
            pltpu.VMEM((rows * cols, CZ), BF16),
            pltpu.VMEM((SL * RB, CM), F32),
            dma((10,)),
            pltpu.VMEM((GPB, CP, LANES), BF16),
            pltpu.VMEM((SL, CP * RB), BF16),
            pltpu.VMEM((SQ, G, CP, LANES), BF16),
            pltpu.VMEM((NB, SQ, SL, CP * RB), BF16),
            pltpu.VMEM((KS, CP * IJ), BF16),
            pltpu.VMEM((G * CP, CP * IJ), BF16),
            pltpu.VMEM((CP * CP, rows * cols), BF16),
            pltpu.VMEM((CP * CP, CZ), F32),
            pltpu.VMEM((CP * CP, CZ), BF16),
            pltpu.VMEM((SQ, G, CP, LANES), BF16),
            pltpu.VMEM((NB, SQ, SL, CP * RB), BF16),
            pltpu.VMEM((C, GPB, CP, LANES), BF16),
            pltpu.VMEM((R * SQ, SL, CP * RB), BF16),
            pltpu.VMEM((2, H, CZ), BF16),
            pltpu.VMEM((H, CZ), BF16),
            pltpu.VMEM((C, H // C, CZ), BF16),
            pltpu.VMEM((C - 1, H // C, CZ), BF16),
            pltpu.VMEM((NZ, H // C, CZ), BF16),
            pltpu.VMEM((2, C, H // C, CZ), BF16),
            pltpu.VMEM((2, CP, CM), BF16),
            pltpu.VMEM((CP, CM), BF16),
            pltpu.VMEM((C, CP, CM), BF16),
            pltpu.VMEM((NZ, CP, CM), BF16),
            pltpu.VMEM((2, CP, CM), BF16),
            dma((1,)),
            dma((1,)),
            dma((1,)),
            dma((1,)),
            dma((1,)),
            dma((1,)),
            dma((1,)),
            dma((1,)),
            dma((10,)),
            dma((8,)),
        ],
        compiler_params=pltpu.CompilerParams(
            collective_id=0, has_side_effects=True, vmem_limit_bytes=56 * 1024 * 1024
        ),
        name="outer_product_mean",
    )(
        alignment.reshape(SL * RB, CM),
        left_weight.T,
        right_weight.T,
        out_weight,
        out_bias.reshape(1, CZ),
        cotangent.reshape(rows * cols, CZ),
    )
    pair, agrad, lwg, rwg, wog = pl.pallas_call(
        finishing,
        out_shape=(
            jax.ShapeDtypeStruct(pair.shape, BF16),
            jax.ShapeDtypeStruct(agrad.shape, F32),
            jax.ShapeDtypeStruct((CP, CM), F32),
            jax.ShapeDtypeStruct((CP, CM), F32),
            jax.ShapeDtypeStruct((CP * CP, CZ), F32),
        ),
        in_specs=[vmem] * 4,
        out_specs=(vmem,) * 5,
        compiler_params=pltpu.CompilerParams(vmem_limit_bytes=56 * 1024 * 1024),
        name="finishing",
    )(pair, agrad, gv, gw)
    return (
        pair.reshape(rows, cols, CZ),
        agrad.reshape(SL, RB, CM),
        lwg.T,
        rwg.T,
        wog,
    )


def solution(mesh):
    placed = (P("seq", ("row", "col"), None), P(), P(), P(), P(), P(("row", "seq"), "col", None))
    return jax.shard_map(
        body,
        mesh=mesh,
        in_specs=placed,
        out_specs=(P(("row", "seq"), "col", None), P("seq", ("row", "col"), None), P(), P(), P()),
        check_vma=False,
    )
```
